256 devices in a mesh: row: 8 (over z), col: 32 (over y, x, core).
Axes of the slice: x: 4, y: 4, z: 8, core: 2. Of those that a mesh axis runs over, the one named last changes fastest.
Arguments:
- states: bfloat16 [524288, 64], P(('row', 'col')), may hold values from -1.5 to 1.5
- right_sides: float32 [17, 524288], P(None, ('row', 'col')), may hold values from -120 to 120
- row_blocks: int32 [256, 320], P(('row', 'col')), may hold values from 0 to 511, as said below
- col_blocks: int32 [256, 320], P(('row', 'col')), may hold values from 0 to 127
- tile_counts: int32 [256], P(('row', 'col')), may hold values from 16 to 320, as said below
Outputs:
- solution: float32 [17, 524288], P(None, ('row', 'col'))
- residual: float32 [17, 524288], P(None, ('row', 'col'))
- direction: float32 [17, 524288], P(None, ('row', 'col'))
The draws below stay inside these ranges and needn't reach their ends.
Inputs may be any that keep to these rules, and one draw needn't show every extreme that they name: `row_blocks`: the kept blocks fall into disjoint groups, and a tile is kept exactly when both of its blocks lie in one group. A device's blocks with local index below 16 / 2 (block g has local index g % 16) group only with blocks of devices of the same row index, and those with local index 8 or more only with blocks of devices of the same col index. Every kept unordered pair of blocks, a block with itself included, is named by exactly one live slot over all devices, in one of its two orders; the two blocks of a live tile lie on different devices unless the tile pairs a block with itself. The mirror (J, I) of a tile belongs to the device whose row index is that of block J's device and whose col index is that of block I's device; the live tiles of a device together with the mirrors of other devices' live tiles that belong to it number at most 320. Slots from tile_counts[d] on hold in-range numbers that name no tile.
All inputs are finite; a program needn't handle non-finite values.
Results may differ from the reference program's by a relative error of at most 0.0044.
Values may be sent and summed in bfloat16 or wider, within the bound.
A program may use at most 128 MiB of HBM per device.

```python
import math
import jax
import jax.numpy as jnp
from jax import lax

FEAT = 64
NV = 17
BLK = 128
SUB = 16
STATES = 524288
MAXT = 320
N_ROW = 8
N_COL = 32
DEVICES = 256


def shuffled(keys, length):

    def permute(single):
        return jax.random.permutation(single, length).astype(jnp.int32)
    return jax.vmap(permute)(keys)


def tile_tables(key):
    key_rows, key_cols, key_subs, key_top, key_order = jax.random.split(key, 5)
    half_sub = SUB // 2
    across_scores = shuffled(jax.random.split(key_rows, N_ROW), N_COL)
    down_scores = shuffled(jax.random.split(key_cols, N_COL), N_ROW).T
    top_keys = jax.random.split(key_top, 2)
    top_row = jax.random.randint(top_keys[0], (), 0, N_ROW)
    top_col = jax.random.randint(top_keys[1], (), 0, N_COL)
    low_row = (top_row + 1) % N_ROW
    low_col = (top_col + 1) % N_COL
    across_scores = across_scores.at[top_row, top_col].set(N_COL).at[low_row, low_col].set(-1)
    down_scores = down_scores.at[top_row, top_col].set(N_ROW).at[low_row, low_col].set(-1)
    across_rank = jnp.argsort(jnp.argsort(across_scores, axis=1), axis=1)
    down_rank = jnp.argsort(jnp.argsort(down_scores, axis=0), axis=0)
    first_order = shuffled(jax.random.split(key_subs, DEVICES), half_sub)
    second_order = shuffled(jax.random.split(jax.random.fold_in(key_subs, 1), DEVICES), half_sub) + half_sub
    sub_order = jnp.concatenate([first_order, second_order], axis=1).reshape(N_ROW, N_COL, SUB)
    here_row = jnp.arange(N_ROW, dtype=jnp.int32)[:, None, None, None]
    here_col = jnp.arange(N_COL, dtype=jnp.int32)[None, :, None, None]
    line_index = jnp.arange(half_sub, dtype=jnp.int32)[None, None, :, None]
    other_col = jnp.arange(N_COL, dtype=jnp.int32)[None, None, None, :]
    other_row = jnp.arange(N_ROW, dtype=jnp.int32)[None, None, None, :]
    full_line = (N_ROW, N_COL, half_sub, N_COL)
    full_stack = (N_ROW, N_COL, half_sub, N_ROW)
    line_rows = jnp.broadcast_to(other_col * SUB + sub_order[here_row, other_col, line_index], full_line)
    line_cols = jnp.broadcast_to(here_row * SUB + sub_order[here_row, here_col, line_index], full_line)
    line_live = jnp.broadcast_to(across_rank[here_row, other_col] <= across_rank[here_row, here_col], full_line)
    stack_rows = jnp.broadcast_to(here_col * SUB + sub_order[here_row, here_col, half_sub + line_index], full_stack)
    stack_cols = jnp.broadcast_to(other_row * SUB + sub_order[other_row, here_col, half_sub + line_index], full_stack)
    stack_live = jnp.broadcast_to(down_rank[other_row, here_col] <= down_rank[here_row, here_col], full_stack)
    rows_all = jnp.concatenate([line_rows.reshape(DEVICES, -1), stack_rows.reshape(DEVICES, -1)], axis=1)
    cols_all = jnp.concatenate([line_cols.reshape(DEVICES, -1), stack_cols.reshape(DEVICES, -1)], axis=1)
    live_all = jnp.concatenate([line_live.reshape(DEVICES, -1), stack_live.reshape(DEVICES, -1)], axis=1).astype(jnp.int32)
    order_scores = (1 - live_all) * MAXT + shuffled(jax.random.split(key_order, DEVICES), MAXT)
    slot_order = jnp.argsort(order_scores, axis=1)
    rows_all = jnp.take_along_axis(rows_all, slot_order, axis=1).astype(jnp.int32)
    cols_all = jnp.take_along_axis(cols_all, slot_order, axis=1).astype(jnp.int32)
    counts = jnp.sum(live_all, axis=1).astype(jnp.int32)
    return (rows_all, cols_all, counts)


def draw_row_blocks(key, part):
    return tile_tables(key)[0]


def draw_col_blocks(key, part):
    return tile_tables(key)[1]


def draw_tile_counts(key, part):
    return tile_tables(key)[2]


def draw_right_sides(key, part):
    key = jax.random.fold_in(key, 7)
    key_base = jax.random.fold_in(key, 0)
    key_rows = jax.random.fold_in(key, 2)
    key_vecs = jax.random.fold_in(key, 3)
    position = jnp.arange(STATES, dtype=jnp.float32) / (STATES - 1)
    ramp = jnp.sqrt(1.0 + 2.0 * position)
    values = jnp.clip(jax.random.normal(key_base, (NV, STATES), jnp.float32), -4.0, 4.0)
    row_scale = jnp.exp(jax.random.uniform(key_rows, (STATES,), jnp.float32, 0.0, math.log(10.0))) / 3.0
    vector_scale = jnp.exp(jax.random.uniform(key_vecs, (NV, 1), jnp.float32, 0.0, math.log(10.0))) / 3.0
    return values * (row_scale * ramp)[None, :] * vector_scale


def steps_of(key, extent, cuts, smallest, top_value):
    loudness, own = 1.0, jax.random.fold_in(key, 6)
    for dim, shards_of in cuts:
        draws = jnp.exp(jax.random.uniform(jax.random.fold_in(own, dim), (shards_of,), jnp.float32, smallest / len(cuts), top_value / len(cuts)))
        loudness = loudness * jnp.repeat(draws, extent[dim] // shards_of).reshape([-1 if axis == dim else 1 for axis in range(len(extent))])
    return loudness


def gaussian(own_key, shape, deviation, bound, cuts=(), kind=jnp.bfloat16):
    level = steps_of(own_key, shape, cuts, -0.22, 0.18) if cuts else 1.0
    result = jax.random.normal(own_key, shape, jnp.float32) * deviation * level
    return jnp.minimum(jnp.maximum(result, -bound), bound).astype(kind)


def setup_inputs(seed: int = 0) -> dict:
    splits = jax.random.split(jax.random.key(seed), 6)
    return {
        "states": gaussian(splits[0], (STATES, FEAT), 0.25, 1.5, ((0, 256),)),
        "right_sides": draw_right_sides(jax.random.fold_in(splits[5], 71), 0),
        "row_blocks": draw_row_blocks(jax.random.fold_in(splits[5], 71), 0),
        "col_blocks": draw_col_blocks(jax.random.fold_in(splits[5], 71), 0),
        "tile_counts": draw_tile_counts(jax.random.fold_in(splits[5], 71), 0),
    }


root_five = math.sqrt(5.0)
noise_level = 1.0

def matern(squared):
    scaled = root_five * jnp.sqrt(jnp.maximum(squared, 0.0))
    return (1.0 + scaled + scaled * scaled / 3.0) * jnp.exp(-scaled)

def reference(states, right_sides, row_blocks, col_blocks, tile_counts):
    block_total = DEVICES * SUB
    stacked = states.reshape(block_total, BLK, FEAT)
    squares = lax.optimization_barrier(jnp.sum(jnp.square(states.astype(jnp.float32)), axis=1)).reshape(block_total, BLK)
    rounded = lax.optimization_barrier(right_sides.astype(jnp.bfloat16))
    vectors = rounded.astype(jnp.float32).reshape(NV, block_total, BLK)
    device = jnp.arange(DEVICES, dtype=jnp.int32)[:, None]
    row_index = device // N_COL
    col_index = device % N_COL
    usable = jnp.arange(MAXT, dtype=jnp.int32)[None, :] < tile_counts[:, None]
    first_block = (row_index * N_COL + row_blocks // SUB) * SUB + row_blocks % SUB
    second_block = (col_blocks // SUB * N_COL + col_index) * SUB + col_blocks % SUB
    slot_total = DEVICES * MAXT
    padded = (slot_total + 63) // 64 * 64
    extra = padded - slot_total
    first_block = jnp.pad(first_block.reshape(-1).astype(jnp.int32), (0, extra)).reshape(-1, 64)
    second_block = jnp.pad(second_block.reshape(-1).astype(jnp.int32), (0, extra)).reshape(-1, 64)
    weights = jnp.pad(usable.reshape(-1).astype(jnp.float32), (0, extra)).reshape(-1, 64)

    def advance(totals, entries):
        first_part, second_part, weight = entries
        left_rows = stacked[first_part].astype(jnp.float32)
        right_rows = stacked[second_part].astype(jnp.float32)
        products = jnp.einsum('tak,tbk->tab', left_rows, right_rows)
        kernel = matern(squares[first_part][:, :, None] + squares[second_part][:, None, :] - 2.0 * products)
        kernel = lax.optimization_barrier(kernel.astype(jnp.bfloat16)).astype(jnp.float32)
        rowwise = jnp.einsum('tab,vtb->vta', kernel, vectors[:, second_part]) * weight[None, :, None]
        mirror = weight * (first_part != second_part).astype(jnp.float32)
        colwise = jnp.einsum('tab,vta->vtb', kernel, vectors[:, first_part]) * mirror[None, :, None]
        totals = totals.at[:, first_part].add(rowwise).at[:, second_part].add(colwise)
        return (totals, None)
    start_totals = jnp.zeros((NV, block_total, BLK), jnp.float32)
    totals, unused = lax.scan(advance, start_totals, (first_block, second_block, weights))
    applied = totals.reshape(NV, -1) + noise_level * right_sides
    old_norm = lax.optimization_barrier(jnp.sum(jnp.square(right_sides), axis=1))
    curvature = lax.optimization_barrier(jnp.sum(right_sides * applied, axis=1))
    step_size = old_norm / curvature
    solution = step_size[:, None] * right_sides
    residual = right_sides - step_size[:, None] * applied
    new_norm = lax.optimization_barrier(jnp.sum(jnp.square(residual), axis=1))
    direction = residual + (new_norm / old_norm)[:, None] * right_sides
    return (solution, residual, direction)
```

```python
import math

import jax
import jax.numpy as jnp
from jax import lax
from jax.experimental import pallas as pl
from jax.experimental.pallas import tpu as pltpu
from jax.sharding import PartitionSpec as P

FEAT = 64
NV = 17
BLK = 128
HALF = 8
N_ROW = 8
N_COL = 32
MAXT = 320

V_AT, W_AT, E_AT, ROWS = 32, 40, 41, 45
PART_A, PART_B = (0, 22), (22, 45)
MESH = pl.DeviceIdType.MESH
NN = (((1,), (0,)), ((), ()))
NT = (((1,), (1,)), ((), ()))
rate = math.sqrt(5.0) * math.log2(math.e)
quad = math.log(2.0) ** 2 / 3.0
lin = math.log(2.0)


def dot(a, b, dims):
    return lax.dot_general(a, b, dims, preferred_element_type=jnp.float32)


def matern(squared):
    kept = jnp.maximum(squared, 1e-30)
    z = (kept * lax.rsqrt(kept)) * (-rate)
    return (((z * quad - lin) * z + 1.0) * jnp.exp2(z)).astype(jnp.bfloat16)


def split3(value):
    high = value.astype(jnp.bfloat16).astype(jnp.float32)
    rest = value - high
    middle = rest.astype(jnp.bfloat16).astype(jnp.float32)
    return high, middle, rest - middle


SOURCE_GROUPS = ((0,), (1, 3), (2,))
PLACE = {dx: (g, 2 * k) for g, group in enumerate(SOURCE_GROUPS) for k, dx in enumerate(group)}
SOURCES = [(dx, dk) for group in SOURCE_GROUPS for dx in group for dk in range(2)]


class Plan:
    def __init__(self):
        self.events = {}
        for m in (1, 3, 2):
            self.add("x%d" % m, "source", 0, (0, ROWS), m)
            self.add("y%d" % m, "output", 0, None, m)
            self.add("r%d" % m, "return", m, None, m)
        for dx in PLACE:
            self.add("s%d" % dx, "sibling", dx, (0, ROWS), 0)
        for step in range(4):
            for part, rows in (("a", PART_A), ("b", PART_B)):
                if step < 3 or part == "a":
                    self.add("u%d%s" % (step + 1, part), "stack", step, rows, 1)
                if step < 3 or part == "b":
                    self.add("d%d%s" % (step + 1, part), "stack", (8 - step) % 8, rows, 7)

    def add(self, name, *what):
        self.events[name] = (len(self.events),) + what


PLAN = Plan()
N_EVENT = len(PLAN.events)


def names(text):
    return text.split()


ROUND0 = names("s0 x1 x3 u1a") + names("d1a u1b d1b y1") + names("y3 x2 y2")
Z1 = [("u1a", "u2a"), ("d1a", "d2a"), ("u1b", "u2b"), ("d1b", "d2b")]
Z2 = [("u2a", "u3a"), ("d2a", "d3a"), ("u2b", "u3b"), ("d2b", "d3b")]
Z3 = [("u3a", "u4a"), ("d3b", "d4b"), ("u3b d3a", "")]


def kernel(
    count_ref, u_ref, v_ref, states_hbm, sides_hbm,
    applied_ref, coef_ref,
    states_ref, sides_ref, buf0, buf1, buf2, bufz, turned_ref, weights, mask_e, mask_v, acc, part_out, part_in,
    mine_ref, theirs_ref, wide_ref, prow, qrow, zrow, qall, ptab, ptab_smem, first_tab, first_smem,
    stat_out, stat1, stat2, stat2_out,
    ssem, rsem, tab_ssem, tab_rsem, st_ssem, st_rsem, local_sem,
):
    z = lax.axis_index("row")
    c = lax.axis_index("col")
    cy, cx, ck = c // 8, (c // 2) % 4, c % 2
    bufs = (buf0, buf1, buf2)
    spot = 2 * cx + ck
    load_states = pltpu.make_async_copy(states_hbm, states_ref, local_sem.at[0])
    load_sides = pltpu.make_async_copy(sides_hbm, sides_ref, local_sem.at[1])
    load_states.start()
    load_sides.start()

    def col_of(dx, dy, dk):
        other = (ck + 1) % 2 if dk else ck
        return (((cy + dy) % 4) * 4 + (cx + dx) % 4) * 2 + other

    barrier = pltpu.get_barrier_semaphore()

    def greet_col(o, carry):
        pl.semaphore_signal(barrier, inc=1, device_id=(z, (c + o) % N_COL), device_id_type=MESH)
        return carry

    def greet_row(o, carry):
        pl.semaphore_signal(barrier, inc=1, device_id=((z + o) % N_ROW, c), device_id_type=MESH)
        return carry

    lax.fori_loop(1, N_COL, greet_col, 0)
    lax.fori_loop(1, N_ROW, greet_row, 0)

    def copy(name):
        index, kind, slot, rows, move = PLAN.events[name]
        span = None if rows is None else pl.ds(rows[0], rows[1] - rows[0])
        if kind == "stack":
            src = bufz.at[slot, span]
            dst = bufz.at[(slot + move) % 8, span]
            target = ((z + move) % N_ROW, c)
        elif kind == "source":
            src = buf0.at[0, span]
            to_g, to_at = PLACE[move]
            dst = bufs[to_g].at[to_at, span]
            target = (z, col_of(move, 0, 0))
        elif kind == "sibling":
            g, at = PLACE[slot]
            src = bufs[g].at[at, span]
            dst = bufs[g].at[at + 1, span]
            target = (z, col_of(0, 0, 1))
        elif kind == "output":
            src = turned_ref.at[0]
            dst = turned_ref.at[move]
            target = (z, col_of(0, move, 0))
        else:
            src = part_out.at[slot - 1]
            dst = part_in.at[slot - 1]
            target = (z, col_of(0, -move, 0))
        return pltpu.make_async_remote_copy(
            src_ref=src, dst_ref=dst, send_sem=ssem.at[index], recv_sem=rsem.at[index],
            device_id=target, device_id_type=MESH,
        )

    def run(entries):
        for waits, starts in entries:
            for name in names(waits):
                copy(name).wait_recv()
            for name in names(starts):
                copy(name).start()

    t16 = lax.broadcasted_iota(jnp.int32, (16, 256), 0)
    n16 = lax.broadcasted_iota(jnp.int32, (16, 256), 1)
    ones16 = ((t16 < 3) & (n16 < 128)) | ((t16 >= 3) & (t16 < 6) & (n16 >= 128))
    ones16 = jnp.where(ones16, 1.0, 0.0).astype(jnp.bfloat16)
    row16 = lax.broadcasted_iota(jnp.int32, (16, 128), 0)
    load_states.wait()
    load_sides.wait()
    lane64 = lax.broadcasted_iota(jnp.int32, (64, 128), 1)
    for base, chunk in ((0, buf0), (HALF, bufz)):
        tail = jnp.where(lane64 % 16 // 3 == 2, 1.0, 0.0)
        for j in range(HALF):
            b = base + j
            turned = states_ref[:, b * BLK:(b + 1) * BLK].astype(jnp.float32)
            own_turned = turned_ref.at[0 if base == 0 else 4, j]
            own_turned[0:4] = (turned * -2.0).astype(jnp.bfloat16).reshape(4, 16, 128)
            small = jnp.zeros((16, 128), jnp.float32)
            for k, piece in enumerate(split3(jnp.sum(turned * turned, axis=0, keepdims=True))):
                small = jnp.where(row16 == 6 + k, piece, small)
            own_turned[4] = small.astype(jnp.bfloat16)
            block = turned.T
            feats = jnp.concatenate([block[:64], block[64:]], axis=1).astype(jnp.bfloat16)
            chunk[0, 4 * j:4 * j + 4] = feats.reshape(4, 16, 128)
            total = jnp.sum(block * block, axis=1, keepdims=True)
            for k, piece in enumerate(split3(total)):
                tail = jnp.where(lane64 == 16 * j + k, piece[:64], tail)
                tail = jnp.where(lane64 == 16 * j + 3 + k, piece[64:], tail)
            sides = sides_ref[:, b * BLK:(b + 1) * BLK]
            chunk[0, V_AT + j] = sides[:16].astype(jnp.bfloat16)
        last = [sides_ref[16:17, (base + j) * BLK:(base + j + 1) * BLK] for j in range(HALF)]
        last = jnp.concatenate(last + [jnp.zeros((8, 128), jnp.float32)], axis=0)
        chunk[0, W_AT] = last.astype(jnp.bfloat16)
        chunk[0, E_AT:E_AT + 4] = tail.astype(jnp.bfloat16).reshape(4, 16, 128)

    u, v = u_ref[...], v_ref[...]
    live = lax.broadcasted_iota(jnp.int32, (1, MAXT), 1) < count_ref[0]
    line = (u & 15) < HALF
    own = jnp.where(line, v & 15, (u & 15) - HALF)
    other = jnp.where(line, u & 15, (v & 15) - HALF)
    partner = jnp.where(live, jnp.where(line, u >> 4, N_COL + (v >> 4)), -1)
    hit = lax.broadcasted_iota(jnp.int32, (40, MAXT), 0) == partner
    lane40 = lax.broadcasted_iota(jnp.int32, (40, 128), 1)
    mine = jnp.zeros((40, 128), jnp.int32)
    theirs = jnp.zeros((40, 128), jnp.int32)
    for i in range(HALF):
        here = jnp.sum(jnp.where(hit & (own == i), other + 1, 0), axis=1, keepdims=True)
        there = jnp.sum(jnp.where(hit & (other == i), own + 1, 0), axis=1, keepdims=True)
        mine = jnp.where(lane40 == i, here, mine)
        theirs = jnp.where(lane40 == i, there, theirs)
    mine_ref[...] = mine
    theirs_ref[...] = theirs[N_COL:]
    wide = theirs[0:8]
    for y in range(1, 4):
        wide = wide + pltpu.roll(theirs[8 * y:8 * y + 8], 8 * y, 1)
    wide_ref[...] = wide
    qrow[spot] = wide
    zrow[z] = theirs[N_COL:]
    prow[0] = mine_ref[pl.ds(pl.multiple_of(8 * cy, 8), 8), :]

    pl.semaphore_wait(barrier, N_COL + N_ROW - 2)

    def share(src_of, dst, ssems, rsems, do_col, do_row, method):
        def col_step(o, carry):
            to = (c + o) % N_COL
            d = pltpu.make_async_remote_copy(
                src_ref=src_of(to), dst_ref=dst.at[c], send_sem=ssems.at[o], recv_sem=rsems.at[o],
                device_id=(z, to), device_id_type=MESH)
            getattr(d, method)()
            return carry

        def row_step(o, carry):
            to = (z + o) % N_ROW
            d = pltpu.make_async_remote_copy(
                src_ref=src_of(do_row + to), dst_ref=dst.at[do_row + z], send_sem=ssems.at[N_COL + o],
                recv_sem=rsems.at[N_COL + o], device_id=(to, c), device_id_type=MESH)
            getattr(d, method)()
            return carry

        if do_col:
            lax.fori_loop(1, N_COL, col_step, 0)
        if do_row is not None:
            lax.fori_loop(1, N_ROW, row_step, 0)

    def table(kind, method):
        if kind == "y":
            moves = [(20 + m, m, 0, 0) for m in (1, 3, 2)]
        elif kind == "x":
            moves = [(2 * m + k, 0, m, k) for m in (1, 3, 2) for k in range(2)]
        elif kind == "sibling":
            moves = [(1, 0, 0, 1)]
        else:
            moves = []
            for o in (4, 3, 5, 2, 6, 1, 7):
                getattr(pltpu.make_async_remote_copy(
                    src_ref=theirs_ref, dst_ref=zrow.at[z], send_sem=tab_ssem.at[8 + o],
                    recv_sem=tab_rsem.at[8 + o], device_id=((z + o) % N_ROW, c),
                    device_id_type=MESH), method)()
        for index, my, mx, mk in moves:
            if kind == "y":
                src = mine_ref.at[pl.ds(pl.multiple_of(8 * ((cy + my) % 4), 8), 8)]
                dst = prow.at[my]
            else:
                src, dst = wide_ref, qrow.at[spot]
            getattr(pltpu.make_async_remote_copy(
                src_ref=src, dst_ref=dst, send_sem=tab_ssem.at[index], recv_sem=tab_rsem.at[index],
                device_id=(z, col_of(mx, my, mk)), device_id_type=MESH), method)()

    KINDS = ("sibling", "x", "y", "z")
    for kind in KINDS:
        table(kind, "start")
    for name in ROUND0:
        copy(name).start()

    zero64 = jnp.zeros((64, 128), jnp.bfloat16)

    def weigh(slot):
        for j in range(HALF):
            at = 8 * slot + j
            scaled = turned_ref[slot, j, 0:4].reshape(64, 128)
            weights[at, 0:64, :] = jnp.concatenate([scaled, zero64], axis=1)
            weights[at, 64:128, :] = jnp.concatenate([zero64, scaled], axis=1)
            strip = turned_ref[slot, j, 4]
            small = jnp.concatenate([strip, strip], axis=1) + ones16
            for k in range(HALF):
                weights[at, 128 + 16 * k:144 + 16 * k, :] = small

    weigh(0)
    weigh(4)
    lane16 = lax.broadcasted_iota(jnp.int32, (16, 128), 1)
    row32 = lax.broadcasted_iota(jnp.int32, (32, 128), 0)
    for p in range(HALF + 1):
        mask_e[p] = jnp.where(lane16 // 16 == p - 1, 1.0, 0.0).astype(jnp.bfloat16)
        keep = (row32 < 16) | (row32 == 16 + p - 1) if p else row32 < 0
        mask_v[p] = jnp.where(keep, 1.0, 0.0).astype(jnp.bfloat16)

    def pairs(dy):
        shift = (128 - 8 * ((cy + 4 - dy) % 4)) % 128
        return jnp.maximum(prow[dy], pltpu.roll(qall[...], shift, 1))

    def source_row(dx, dk):
        return 2 * ((cx + 4 - dx) % 4) + ((ck + 1) % 2 if dk else ck)

    def group(sources, base, tab, rows, put, inside):
        def one(i):
            right = weights[base + i]
            parts, sides = [], []
            for s in range(len(rows)):
                buf, slot = sources[s]
                p = tab[rows[s], i]
                at = jnp.maximum(p - 1, 0)
                chosen = mask_e[p]
                for k in range(4):
                    parts.append(jnp.concatenate([buf[slot, at * 4 + k], buf[slot, E_AT + k] * chosen], axis=1))
                sides.append(jnp.concatenate([buf[slot, V_AT + at], buf[slot, W_AT]], axis=0) * mask_v[p])
            tiles = matern(dot(jnp.concatenate(parts, axis=0), right, NN))
            stacked = [
                tiles[64 * s:64 * s + 64, 128 * h:128 * h + 128] for s in range(len(rows)) for h in range(2)
            ]
            out = dot(jnp.concatenate(sides, axis=1), jnp.concatenate(stacked, axis=0), NN)
            last = jnp.sum(out[16:24], axis=0, keepdims=True)
            put(i, jnp.concatenate([out[:16], jnp.broadcast_to(last, (8, 128))], axis=0))

        def body(turn, carry):
            for at, entries in inside.items():
                @pl.when(turn == at)
                def _():
                    run(entries)
            one(2 * turn)
            one(2 * turn + 1)
            return carry

        lax.fori_loop(0, HALF // 2, body, 0)

    def put_own(base, first):
        def put(i, out):
            if first:
                acc[base + i] = out
            else:
                acc[base + i] += out
        return put

    def put_part(dy):
        def put(i, out):
            part_out[dy - 1, i] = out
        return put

    def of_group(g):
        return [(bufs[g], at) for at in range(2 * len(SOURCE_GROUPS[g]))]

    def rows_of(g):
        return [source_row(dx, dk) for dx in SOURCE_GROUPS[g] for dk in range(2)]

    for row in range(8):
        qall[row:row + 1, :] = jnp.zeros((1, 128), jnp.int32)
    sibling_row = source_row(0, 1)
    table("sibling", "wait_recv")
    qall[pl.ds(spot, 1), :] = qrow[spot, pl.ds(spot, 1), :]
    qall[pl.ds(sibling_row, 1), :] = qrow[sibling_row, pl.ds(spot, 1), :]
    first_tab[...] = pairs(0)
    to_smem = pltpu.make_async_copy(first_tab, first_smem, local_sem.at[0])
    to_smem.start()
    to_smem.wait()
    run([("s0", "")])
    group(of_group(0), 0, first_smem, rows_of(0), put_own(0, True), {})

    for kind in ("x", "y", "z"):
        table(kind, "wait_recv")
    for row in range(8):
        qall[row:row + 1, :] = qrow[row, pl.ds(spot, 1), :]
    for dy in range(4):
        ptab[8 * dy:8 * dy + 8, :] = pairs(dy)
    for row in range(8):
        qall[row:row + 1, :] = zrow[row, pl.ds(z, 1), :]
    ptab[N_COL:, :] = jnp.maximum(mine_ref[N_COL:, :], qall[...])
    to_smem = pltpu.make_async_copy(ptab, ptab_smem, local_sem.at[0])
    to_smem.start()
    to_smem.wait()

    run([("x1", "s1"), ("x3", "s3")] + Z1 + [("s1 s3", "")])
    group(of_group(1), 0, ptab_smem, rows_of(1), put_own(0, False), {3: [("x2", "s2")]})
    run([("s2", "")])
    group(of_group(2), 0, ptab_smem, rows_of(2), put_own(0, False), {1: Z2})
    everything = of_group(0) + of_group(1) + of_group(2)
    all_rows = rows_of(0) + rows_of(1) + rows_of(2)
    for dy, inside in ((1, {}), (3, {0: Z3}), (2, {})):
        run([("y%d" % dy, "")])
        weigh(dy)
        group(everything, 8 * dy, ptab_smem, [8 * dy + row for row in all_rows], put_part(dy), inside)
        run([("", "r%d" % dy)])
    run([("u4a d4b", "")])
    stack_rows = [N_COL + (z + N_ROW - d) % N_ROW for d in range(N_ROW)]
    group([(bufz, d) for d in range(N_ROW)], 4 * HALF, ptab_smem, stack_rows, put_own(HALF, True), {})
    run([("r1 r3 r2", "")])

    old = jnp.zeros((NV, 128), jnp.float32)
    curve = jnp.zeros((NV, 128), jnp.float32)
    for b in range(2 * HALF):
        product = acc[b]
        if b < HALF:
            product = product + part_in[0, b] + part_in[1, b] + part_in[2, b]
        sides = sides_ref[:, b * BLK:(b + 1) * BLK]
        applied = sides + product[:NV]
        applied_ref[:, b * BLK:(b + 1) * BLK] = applied
        old += sides * sides
        curve += sides * applied
    old = jnp.sum(old, axis=1, keepdims=True)
    curve = jnp.sum(curve, axis=1, keepdims=True)
    centre = jnp.where(curve > 0.0, jnp.minimum(old / curve, 1.0), 1.0)
    n_sum = jnp.zeros((NV, 128), jnp.float32)
    d_sum = jnp.zeros((NV, 128), jnp.float32)
    q_sum = jnp.zeros((NV, 128), jnp.float32)
    for b in range(2 * HALF):
        applied = applied_ref[:, b * BLK:(b + 1) * BLK]
        left = sides_ref[:, b * BLK:(b + 1) * BLK] - centre * applied
        n_sum += left * left
        d_sum += left * applied
        q_sum += applied * applied
    columns = [old, curve] + [jnp.sum(s, axis=1, keepdims=True) for s in (n_sum, d_sum, q_sum)] + [centre]
    lane17 = lax.broadcasted_iota(jnp.int32, (NV, 128), 1)
    packed = jnp.zeros((NV, 128), jnp.float32)
    for k, column in enumerate(columns):
        packed = jnp.where(lane17 == k, column, packed)
    packed = jnp.concatenate([packed, jnp.zeros((128 - NV, 128), jnp.float32)], axis=0)
    mine_stats = packed.T[0:8]

    def merge(stats):
        total = jnp.sum(stats, axis=0)
        old, curve, q = total[0:1], total[1:2], total[4:5]
        ratio = old / curve
        centre = jnp.where(curve > 0.0, jnp.minimum(ratio, 1.0), 1.0)

        def moved(to):
            eps = to - stats[:, 5:6, :]
            n = stats[:, 2:3, :] - 2.0 * eps * stats[:, 3:4, :] + eps * eps * stats[:, 4:5, :]
            return jnp.sum(n, axis=0), jnp.sum(stats[:, 3:4, :] - eps * stats[:, 4:5, :], axis=0)

        return old, curve, q, ratio, centre, moved

    stat_out[...] = mine_stats
    stat1[c] = mine_stats
    share(lambda at: stat_out, stat1, st_ssem, st_rsem, True, None, "start")
    share(lambda at: stat_out, stat1, st_ssem, st_rsem, True, None, "wait_recv")
    old, curve, q, ratio, centre, moved = merge(stat1[...])
    n, d = moved(centre)
    row_stats = jnp.concatenate([old, curve, n, d, q, centre, old, old], axis=0)
    stat2_out[...] = row_stats
    stat2[z] = row_stats
    share(lambda at: stat2_out, stat2, st_ssem, st_rsem, False, 0, "start")
    share(lambda at: stat2_out, stat2, st_ssem, st_rsem, False, 0, "wait_recv")
    old, curve, q, ratio, centre, moved = merge(stat2[...])
    n, d = moved(ratio)
    pair = jnp.concatenate([ratio, n / old, jnp.zeros((126, 128), jnp.float32)], axis=0)
    coef_ref[...] = pair.T[0:24]

    for name in PLAN.events:
        copy(name).wait_send()
    for kind in KINDS:
        table(kind, "wait_send")
    share(lambda at: stat_out, stat1, st_ssem, st_rsem, True, None, "wait_send")
    share(lambda at: stat2_out, stat2, st_ssem, st_rsem, False, 0, "wait_send")


def iterate(states, right_sides, row_blocks, col_blocks, tile_counts):
    vmem = pl.BlockSpec(memory_space=pltpu.VMEM)
    hbm = pl.BlockSpec(memory_space=pltpu.HBM)
    sizes = [2 * len(group) for group in SOURCE_GROUPS] + [N_ROW]
    table = pltpu.VMEM((8, 128), jnp.int32)
    return pl.pallas_call(
        kernel,
        out_shape=(
            jax.ShapeDtypeStruct((NV, 2048), jnp.float32),
            jax.ShapeDtypeStruct((24, 128), jnp.float32),
        ),
        in_specs=[pl.BlockSpec(memory_space=pltpu.SMEM), vmem, vmem, hbm, hbm],
        out_specs=(vmem, vmem),
        scratch_shapes=[
            pltpu.VMEM((FEAT, 2048), jnp.bfloat16),
            pltpu.VMEM((NV, 2048), jnp.float32),
        ] + [pltpu.VMEM((n, ROWS, 16, 128), jnp.bfloat16) for n in sizes] + [
            pltpu.VMEM((5, HALF, 5, 16, 128), jnp.bfloat16),
            pltpu.VMEM((5 * HALF, 256, 256), jnp.bfloat16),
            pltpu.VMEM((HALF + 1, 16, 128), jnp.bfloat16),
            pltpu.VMEM((HALF + 1, 32, 128), jnp.bfloat16),
            pltpu.VMEM((2 * HALF, 24, 128), jnp.float32),
            pltpu.VMEM((3, HALF, 24, 128), jnp.float32),
            pltpu.VMEM((3, HALF, 24, 128), jnp.float32),
            pltpu.VMEM((40, 128), jnp.int32),
            table,
            table,
            pltpu.VMEM((4, 8, 128), jnp.int32),
            pltpu.VMEM((8, 8, 128), jnp.int32),
            pltpu.VMEM((8, 8, 128), jnp.int32),
            table,
            pltpu.VMEM((40, 128), jnp.int32),
            pltpu.SMEM((40, 128), jnp.int32),
            table,
            pltpu.SMEM((8, 128), jnp.int32),
            pltpu.VMEM((8, 128), jnp.float32),
            pltpu.VMEM((N_COL, 8, 128), jnp.float32),
            pltpu.VMEM((N_ROW, 8, 128), jnp.float32),
            pltpu.VMEM((8, 128), jnp.float32),
            pltpu.SemaphoreType.DMA((N_EVENT,)),
            pltpu.SemaphoreType.DMA((N_EVENT,)),
            pltpu.SemaphoreType.DMA((N_COL + N_ROW,)),
            pltpu.SemaphoreType.DMA((N_COL + N_ROW,)),
            pltpu.SemaphoreType.DMA((N_COL + N_ROW,)),
            pltpu.SemaphoreType.DMA((N_COL + N_ROW,)),
            pltpu.SemaphoreType.DMA((2,)),
        ],
        compiler_params=pltpu.CompilerParams(
            collective_id=0, has_side_effects=True, vmem_limit_bytes=40 * 1024 * 1024
        ),
        name="gather_apply_reduce",
    )(tile_counts, row_blocks, col_blocks, states.T, right_sides)


def shards(states, right_sides, row_blocks, col_blocks, tile_counts):
    applied, coef = iterate(states, right_sides, row_blocks, col_blocks, tile_counts)
    step_size, ratio = coef[:NV, 0:1], coef[:NV, 1:2]
    residual = right_sides - step_size * applied
    return (step_size * right_sides, residual, residual + ratio * right_sides)


def solution(mesh):
    placed = (
        P(("row", "col"), None),
        P(None, ("row", "col")),
        P(("row", "col"), None),
        P(("row", "col"), None),
        P(("row", "col")),
    )
    return jax.shard_map(
        shards,
        mesh=mesh,
        in_specs=placed,
        out_specs=(P(None, ("row", "col")), P(None, ("row", "col")), P(None, ("row", "col"))),
        check_vma=False,
    )
```

```python
import math

import jax
import jax.numpy as jnp
from jax import lax
from jax.experimental import pallas as pl
from jax.experimental.pallas import tpu as pltpu
from jax.sharding import PartitionSpec as P

FEAT = 64
NV = 17
BLK = 128
HALF = 8
N_ROW = 8
N_COL = 32
MAXT = 320

V_AT, W_AT, E_AT, ROWS = 32, 40, 41, 45
PART_A, PART_B = (0, 22), (22, 45)
MESH = pl.DeviceIdType.MESH
COL_ORDER = [*range(16, 24), *range(8, 16), *range(1, 8), *range(24, 32)]
ROW_ORDER = [4, 3, 5, 2, 6, 1, 7]
NN = (((1,), (0,)), ((), ()))
NT = (((1,), (1,)), ((), ()))
rate = math.sqrt(5.0) * math.log2(math.e)
quad = math.log(2.0) ** 2 / 3.0
lin = math.log(2.0)


def dot(a, b, dims):
    return lax.dot_general(a, b, dims, preferred_element_type=jnp.float32)


def matern(squared):
    kept = jnp.maximum(squared, 1e-30)
    z = (kept * lax.rsqrt(kept)) * (-rate)
    return (((z * quad - lin) * z + 1.0) * jnp.exp2(z)).astype(jnp.bfloat16)


def split3(value):
    high = value.astype(jnp.bfloat16).astype(jnp.float32)
    rest = value - high
    middle = rest.astype(jnp.bfloat16).astype(jnp.float32)
    return high, middle, rest - middle


SOURCE_GROUPS = ((0,), (1, 3), (2,))
OUTPUTS = (0, 1, 3, 2)
STACK = 4
PLACE = {dx: (g, 2 * k) for g, group in enumerate(SOURCE_GROUPS) for k, dx in enumerate(group)}


class Plan:
    def __init__(self):
        self.events = {}
        for m in (1, 3, 2):
            self.add("x%d" % m, "source", 0, (0, ROWS), m)
            self.add("y%d" % m, "output", 0, None, m)
            self.add("r%d" % m, "return", m, None, m)
        for dx in PLACE:
            self.add("s%d" % dx, "sibling", dx, (0, ROWS), 0)
        for step in range(4):
            for part, rows in (("a", PART_A), ("b", PART_B)):
                if step < 3 or part == "a":
                    self.add("u%d%s" % (step + 1, part), "stack", step, rows, 1)
                if step < 3 or part == "b":
                    self.add("d%d%s" % (step + 1, part), "stack", (8 - step) % 8, rows, 7)

    def add(self, name, *what):
        self.events[name] = (len(self.events),) + what


PLAN = Plan()
N_EVENT = len(PLAN.events)


def names(text):
    return text.split()


ROUND0 = names("s0 x1 x3 y1") + names("y3 u1a d1a") + names("u1b d1b")
Z1 = [("u1a", "u2a"), ("d1a", "d2a"), ("u1b", "u2b"), ("d1b", "d2b")]
Z2 = [("u2a", "u3a"), ("d2a", "d3a"), ("u2b", "u3b"), ("d2b", "d3b")]
Z3 = [("u3a", "u4a"), ("d3b", "d4b"), ("u3b d3a", "")]


def kernel(
    count_ref, u_hbm, v_hbm, states_hbm, sides_hbm,
    applied_ref, coef_ref,
    u_ref, v_ref, states_ref, sides_ref, buf0, buf1, buf2, bufz, turned_ref, weights, mask_e, mask_v, acc, part_in,
    mine_ref, theirs_ref, wide_ref, prow, qrow, zrow, qall, ptab, ptab_smem, first_tab, first_smem, last_tab, last_smem,
    stat_out, stat1, stat2, stat2_out,
    ssem, rsem, tab_ssem, tab_rsem, st_ssem, st_rsem, local_sem,
):
    z = lax.axis_index("row")
    c = lax.axis_index("col")
    cy, cx, ck = c // 8, (c // 2) % 4, c % 2
    bufs = (buf0, buf1, buf2)
    spot = 2 * cx + ck
    load_states = pltpu.make_async_copy(states_hbm, states_ref, local_sem.at[0])
    load_sides = pltpu.make_async_copy(sides_hbm, sides_ref, local_sem.at[1])
    load_u = pltpu.make_async_copy(u_hbm, u_ref, local_sem.at[2])
    load_v = pltpu.make_async_copy(v_hbm, v_ref, local_sem.at[3])
    load_states.start()
    load_sides.start()
    load_u.start()
    load_v.start()

    def col_of(dx, dy, dk):
        other = (ck + 1) % 2 if dk else ck
        return (((cy + dy) % 4) * 4 + (cx + dx) % 4) * 2 + other

    barrier = pltpu.get_barrier_semaphore()

    def greet_col(o, carry):
        pl.semaphore_signal(barrier, inc=1, device_id=(z, (c + o) % N_COL), device_id_type=MESH)
        return carry

    def greet_row(o, carry):
        pl.semaphore_signal(barrier, inc=1, device_id=((z + o) % N_ROW, c), device_id_type=MESH)
        return carry

    lax.fori_loop(1, N_COL, greet_col, 0)
    lax.fori_loop(1, N_ROW, greet_row, 0)

    def copy(name):
        index, kind, slot, rows, move = PLAN.events[name]
        span = None if rows is None else pl.ds(rows[0], rows[1] - rows[0])
        if kind == "stack":
            src = bufz.at[slot, span]
            dst = bufz.at[(slot + move) % 8, span]
            target = ((z + move) % N_ROW, c)
        elif kind == "source":
            src = buf0.at[0, span]
            to_g, to_at = PLACE[move]
            dst = bufs[to_g].at[to_at, span]
            target = (z, col_of(move, 0, 0))
        elif kind == "sibling":
            g, at = PLACE[slot]
            src = bufs[g].at[at, span]
            dst = bufs[g].at[at + 1, span]
            target = (z, col_of(0, 0, 1))
        elif kind == "output":
            src = turned_ref.at[0]
            dst = turned_ref.at[OUTPUTS.index(move)]
            target = (z, col_of(0, move, 0))
        else:
            src = acc.at[pl.ds(8 * OUTPUTS.index(slot), 8)]
            dst = part_in.at[OUTPUTS.index(slot) - 1]
            target = (z, col_of(0, -move, 0))
        return pltpu.make_async_remote_copy(
            src_ref=src, dst_ref=dst, send_sem=ssem.at[index], recv_sem=rsem.at[index],
            device_id=target, device_id_type=MESH,
        )

    def run(entries):
        for waits, starts in entries:
            for name in names(waits):
                copy(name).wait_recv()
            for name in names(starts):
                copy(name).start()

    t16 = lax.broadcasted_iota(jnp.int32, (16, 256), 0)
    n16 = lax.broadcasted_iota(jnp.int32, (16, 256), 1)
    ones16 = ((t16 < 3) & (n16 < 128)) | ((t16 >= 3) & (t16 < 6) & (n16 >= 128))
    ones16 = jnp.where(ones16, 1.0, 0.0).astype(jnp.bfloat16)
    row16 = lax.broadcasted_iota(jnp.int32, (16, 128), 0)
    load_states.wait()
    load_sides.wait()
    lane64 = lax.broadcasted_iota(jnp.int32, (64, 128), 1)
    for base, chunk in ((0, buf0), (HALF, bufz)):
        tail = jnp.where(lane64 % 16 // 3 == 2, 1.0, 0.0)
        for j in range(HALF):
            b = base + j
            turned = states_ref[:, b * BLK:(b + 1) * BLK].astype(jnp.float32)
            own_turned = turned_ref.at[0 if base == 0 else STACK, j]
            own_turned[0:4] = (turned * -2.0).astype(jnp.bfloat16).reshape(4, 16, 128)
            small = jnp.zeros((16, 128), jnp.float32)
            for k, piece in enumerate(split3(jnp.sum(turned * turned, axis=0, keepdims=True))):
                small = jnp.where(row16 == 6 + k, piece, small)
            own_turned[4] = small.astype(jnp.bfloat16)
            block = turned.T
            feats = jnp.concatenate([block[:64], block[64:]], axis=1).astype(jnp.bfloat16)
            chunk[0, 4 * j:4 * j + 4] = feats.reshape(4, 16, 128)
            total = jnp.sum(block * block, axis=1, keepdims=True)
            for k, piece in enumerate(split3(total)):
                tail = jnp.where(lane64 == 16 * j + k, piece[:64], tail)
                tail = jnp.where(lane64 == 16 * j + 3 + k, piece[64:], tail)
            sides = sides_ref[:, b * BLK:(b + 1) * BLK]
            chunk[0, V_AT + j] = sides[:16].astype(jnp.bfloat16)
        last = [sides_ref[16:17, (base + j) * BLK:(base + j + 1) * BLK] for j in range(HALF)]
        last = jnp.concatenate(last + [jnp.zeros((8, 128), jnp.float32)], axis=0)
        chunk[0, W_AT] = last.astype(jnp.bfloat16)
        chunk[0, E_AT:E_AT + 4] = tail.astype(jnp.bfloat16).reshape(4, 16, 128)

    load_u.wait()
    load_v.wait()
    u, v = u_ref[...], v_ref[...]
    live = lax.broadcasted_iota(jnp.int32, (1, MAXT), 1) < count_ref[0]
    line = (u & 15) < HALF
    own = jnp.where(line, v & 15, (u & 15) - HALF)
    other = jnp.where(line, u & 15, (v & 15) - HALF)
    partner = jnp.where(live, jnp.where(line, u >> 4, N_COL + (v >> 4)), -1)
    hit = lax.broadcasted_iota(jnp.int32, (40, MAXT), 0) == partner
    lane40 = lax.broadcasted_iota(jnp.int32, (40, 128), 1)
    mine = jnp.zeros((40, 128), jnp.int32)
    theirs = jnp.zeros((40, 128), jnp.int32)
    for i in range(HALF):
        here = jnp.sum(jnp.where(hit & (own == i), other + 1, 0), axis=1, keepdims=True)
        there = jnp.sum(jnp.where(hit & (other == i), own + 1, 0), axis=1, keepdims=True)
        mine = jnp.where(lane40 == i, here, mine)
        theirs = jnp.where(lane40 == i, there, theirs)
    mine_ref[...] = mine
    theirs_ref[...] = theirs[N_COL:]
    wide = theirs[0:8]
    for y in range(1, 4):
        wide = wide + pltpu.roll(theirs[8 * y:8 * y + 8], 8 * y, 1)
    wide_ref[...] = wide
    qrow[spot] = wide
    zrow[z] = theirs[N_COL:]
    prow[0] = mine_ref[pl.ds(pl.multiple_of(8 * cy, 8), 8), :]

    zero64 = jnp.zeros((64, 128), jnp.bfloat16)

    def weigh(slot):
        for j in range(HALF):
            at = 8 * slot + j
            scaled = turned_ref[slot, j, 0:4].reshape(64, 128)
            weights[at, 0:64, :] = jnp.concatenate([scaled, zero64], axis=1)
            weights[at, 64:128, :] = jnp.concatenate([zero64, scaled], axis=1)
            strip = turned_ref[slot, j, 4]
            small = jnp.concatenate([strip, strip], axis=1) + ones16
            for k in range(HALF):
                weights[at, 128 + 16 * k:144 + 16 * k, :] = small

    weigh(0)
    lane16 = lax.broadcasted_iota(jnp.int32, (16, 128), 1)
    row32 = lax.broadcasted_iota(jnp.int32, (32, 128), 0)
    for p in range(HALF + 1):
        mask_e[p] = jnp.where(lane16 // 16 == p - 1, 1.0, 0.0).astype(jnp.bfloat16)
        keep = (row32 < 16) | (row32 == 16 + p - 1) if p else row32 < 0
        mask_v[p] = jnp.where(keep, 1.0, 0.0).astype(jnp.bfloat16)

    pl.semaphore_wait(barrier, N_COL + N_ROW - 2)

    def share(src, dst, along_col, method):
        offsets = COL_ORDER if along_col else ROW_ORDER
        for o in offsets:
            if along_col:
                to, slot, sem = (z, (c + o) % N_COL), c, o
            else:
                to, slot, sem = ((z + o) % N_ROW, c), z, N_COL + o
            d = pltpu.make_async_remote_copy(
                src_ref=src, dst_ref=dst.at[slot], send_sem=st_ssem.at[sem], recv_sem=st_rsem.at[sem],
                device_id=to, device_id_type=MESH)
            getattr(d, method)()

    def table(kind, method):
        if kind == "y":
            moves = [(20 + m, m, 0, 0) for m in (1, 3, 2)]
        elif kind == "x":
            moves = [(2 * m + k, 0, m, k) for m in (1, 3, 2) for k in range(2)]
        elif kind == "sibling":
            moves = [(1, 0, 0, 1)]
        else:
            moves = []
            for o in (4, 3, 5, 2, 6, 1, 7):
                getattr(pltpu.make_async_remote_copy(
                    src_ref=theirs_ref, dst_ref=zrow.at[z], send_sem=tab_ssem.at[8 + o],
                    recv_sem=tab_rsem.at[8 + o], device_id=((z + o) % N_ROW, c),
                    device_id_type=MESH), method)()
        for index, my, mx, mk in moves:
            if kind == "y":
                src = mine_ref.at[pl.ds(pl.multiple_of(8 * ((cy + my) % 4), 8), 8)]
                dst = prow.at[my]
            else:
                src, dst = wide_ref, qrow.at[spot]
            getattr(pltpu.make_async_remote_copy(
                src_ref=src, dst_ref=dst, send_sem=tab_ssem.at[index], recv_sem=tab_rsem.at[index],
                device_id=(z, col_of(mx, my, mk)), device_id_type=MESH), method)()

    KINDS = ("sibling", "x", "y", "z")
    for kind in KINDS:
        table(kind, "start")
    for name in ROUND0:
        copy(name).start()

    def pairs(dy):
        shift = (128 - 8 * ((cy + 4 - dy) % 4)) % 128
        return jnp.maximum(prow[dy], pltpu.roll(qall[...], shift, 1))

    def source_row(dx, dk):
        return 2 * ((cx + 4 - dx) % 4) + ((ck + 1) % 2 if dk else ck)

    def group(sources, tab, rows, base, outputs, add, unroll, inside):
        def one(i):
            right = weights[base + i]
            first_row = 0 if base == STACK * HALF else base + i - i % HALF
            parts, sides = [], []
            for (buf, slot), row in zip(sources, rows):
                p = tab[row + first_row, i % HALF]
                at = jnp.maximum(p - 1, 0)
                chosen = mask_e[p]
                for k in range(4):
                    parts.append(jnp.concatenate([buf[slot, at * 4 + k], buf[slot, E_AT + k] * chosen], axis=1))
                sides.append(jnp.concatenate([buf[slot, V_AT + at], buf[slot, W_AT]], axis=0) * mask_v[p])
            tiles = matern(dot(jnp.concatenate(parts, axis=0), right, NN))
            stacked = [
                tiles[64 * s:64 * s + 64, 128 * h:128 * h + 128] for s in range(len(sources)) for h in range(2)
            ]
            out = dot(jnp.concatenate(sides, axis=1), jnp.concatenate(stacked, axis=0), NN)
            last = jnp.sum(out[16:24], axis=0, keepdims=True)
            out = jnp.concatenate([out[:16], jnp.broadcast_to(last, (8, 128))], axis=0)
            if add:
                acc[base + i] += out
            else:
                acc[base + i] = out

        def body(turn, carry):
            for at, entries in inside.items():
                @pl.when(turn == at)
                def _():
                    run(entries)
            for step in range(unroll):
                one(unroll * turn + step)
            return carry

        lax.fori_loop(0, outputs * HALF // unroll, body, 0)

    def of_groups(*which):
        sources = [(bufs[g], at) for g in which for at in range(2 * len(SOURCE_GROUPS[g]))]
        rows = [source_row(dx, dk) for g in which for dx in SOURCE_GROUPS[g] for dk in range(2)]
        return sources, rows

    for row in range(8):
        qall[row:row + 1, :] = jnp.zeros((1, 128), jnp.int32)
    sibling_row = source_row(0, 1)
    table("sibling", "wait_recv")
    qall[pl.ds(spot, 1), :] = qrow[spot, pl.ds(spot, 1), :]
    qall[pl.ds(sibling_row, 1), :] = qrow[sibling_row, pl.ds(spot, 1), :]
    first_tab[...] = pairs(0)
    to_smem = pltpu.make_async_copy(first_tab, first_smem, local_sem.at[0])
    to_smem.start()
    to_smem.wait()
    run([("s0", "")])
    sources, rows = of_groups(0)
    group(sources, first_smem, rows, 0, 1, False, 8, {})
    run([("", "x2 y2")])

    for kind in ("x", "y"):
        table(kind, "wait_recv")
    for row in range(8):
        qall[row:row + 1, :] = qrow[row, pl.ds(spot, 1), :]
    for k, dy in enumerate(OUTPUTS):
        ptab[8 * k:8 * k + 8, :] = pairs(dy)
    to_smem = pltpu.make_async_copy(ptab, ptab_smem, local_sem.at[0])
    to_smem.start()
    to_smem.wait()
    weigh(STACK)

    run([("x1", "s1"), ("x3", "s3")] + Z1 + [("s1 s3", "")])
    sources, rows = of_groups(1)
    group(sources, ptab_smem, rows, 0, 1, True, 4, {})

    table("z", "wait_recv")
    for row in range(8):
        qall[row:row + 1, :] = zrow[row, pl.ds(z, 1), :]
    last_tab[...] = jnp.maximum(mine_ref[N_COL:, :], qall[...])
    to_smem = pltpu.make_async_copy(last_tab, last_smem, local_sem.at[1])
    to_smem.start()

    run([("y1 y3", "")])
    weigh(1)
    weigh(2)
    sources, rows = of_groups(0, 1)
    group(sources, ptab_smem, rows, HALF, 2, False, 4, {1: [("x2", "s2")], 2: Z2})
    run([("s2 y2", "")])
    weigh(3)
    sources, rows = of_groups(2)
    last_sources, last_rows = sources, rows
    group(sources, ptab_smem, rows, HALF, 2, True, 8, {})
    run([("", "r1 r3")] + Z3)
    sources, rows = of_groups(0, 1, 2)
    group(sources, ptab_smem, rows, 3 * HALF, 1, False, 4, {})
    run([("", "r2")])
    group(last_sources, ptab_smem, last_rows, 0, 1, True, 8, {})
    run([("u4a d4b", "")])
    to_smem.wait()
    stack_rows = [(z + N_ROW - d) % N_ROW for d in range(N_ROW)]
    group([(bufz, d) for d in range(N_ROW)], last_smem, stack_rows, STACK * HALF, 1, False, 4, {})
    run([("r1 r3 r2", "")])

    old = jnp.zeros((NV, 128), jnp.float32)
    curve = jnp.zeros((NV, 128), jnp.float32)
    for b in range(2 * HALF):
        product = acc[b if b < HALF else STACK * HALF + b - HALF]
        if b < HALF:
            product = product + part_in[0, b] + part_in[1, b] + part_in[2, b]
        sides = sides_ref[:, b * BLK:(b + 1) * BLK]
        applied = sides + product[:NV]
        applied_ref[:, b * BLK:(b + 1) * BLK] = applied
        old += sides * sides
        curve += sides * applied
    old = jnp.sum(old, axis=1, keepdims=True)
    curve = jnp.sum(curve, axis=1, keepdims=True)
    centre = jnp.where(curve > 0.0, jnp.minimum(old / curve, 1.0), 1.0)
    n_sum = jnp.zeros((NV, 128), jnp.float32)
    d_sum = jnp.zeros((NV, 128), jnp.float32)
    q_sum = jnp.zeros((NV, 128), jnp.float32)
    for b in range(2 * HALF):
        applied = applied_ref[:, b * BLK:(b + 1) * BLK]
        left = sides_ref[:, b * BLK:(b + 1) * BLK] - centre * applied
        n_sum += left * left
        d_sum += left * applied
        q_sum += applied * applied
    columns = [old, curve] + [jnp.sum(s, axis=1, keepdims=True) for s in (n_sum, d_sum, q_sum)] + [centre]
    lane17 = lax.broadcasted_iota(jnp.int32, (NV, 128), 1)
    packed = jnp.zeros((NV, 128), jnp.float32)
    for k, column in enumerate(columns):
        packed = jnp.where(lane17 == k, column, packed)
    packed = jnp.concatenate([packed, jnp.zeros((128 - NV, 128), jnp.float32)], axis=0)
    mine_stats = packed.T[0:8]

    def merge(stats):
        total = jnp.sum(stats, axis=0)
        old, curve, q = total[0:1], total[1:2], total[4:5]
        ratio = old / curve
        centre = jnp.where(curve > 0.0, jnp.minimum(ratio, 1.0), 1.0)

        def moved(to):
            eps = to - stats[:, 5:6, :]
            n = stats[:, 2:3, :] - 2.0 * eps * stats[:, 3:4, :] + eps * eps * stats[:, 4:5, :]
            return jnp.sum(n, axis=0), jnp.sum(stats[:, 3:4, :] - eps * stats[:, 4:5, :], axis=0)

        return old, curve, q, ratio, centre, moved

    stat_out[...] = mine_stats
    stat1[c] = mine_stats
    share(stat_out, stat1, True, "start")
    for name in PLAN.events:
        copy(name).wait_send()
    for kind in KINDS:
        table(kind, "wait_send")
    share(stat_out, stat1, True, "wait_recv")
    old, curve, q, ratio, centre, moved = merge(stat1[...])
    n, d = moved(centre)
    row_stats = jnp.concatenate([old, curve, n, d, q, centre, old, old], axis=0)
    stat2_out[...] = row_stats
    stat2[z] = row_stats
    share(stat2_out, stat2, False, "start")
    share(stat_out, stat1, True, "wait_send")
    share(stat2_out, stat2, False, "wait_recv")
    old, curve, q, ratio, centre, moved = merge(stat2[...])
    n, d = moved(ratio)
    pair = jnp.concatenate([ratio, n / old, jnp.zeros((126, 128), jnp.float32)], axis=0)
    coef_ref[...] = pair.T[0:24]

    share(stat2_out, stat2, False, "wait_send")


def iterate(states, right_sides, row_blocks, col_blocks, tile_counts):
    vmem = pl.BlockSpec(memory_space=pltpu.VMEM)
    hbm = pl.BlockSpec(memory_space=pltpu.HBM)
    sizes = [2 * len(group) for group in SOURCE_GROUPS] + [N_ROW]
    table = pltpu.VMEM((8, 128), jnp.int32)
    return pl.pallas_call(
        kernel,
        out_shape=(
            jax.ShapeDtypeStruct((NV, 2048), jnp.float32),
            jax.ShapeDtypeStruct((24, 128), jnp.float32),
        ),
        in_specs=[pl.BlockSpec(memory_space=pltpu.SMEM), hbm, hbm, hbm, hbm],
        out_specs=(vmem, vmem),
        scratch_shapes=[
            pltpu.VMEM((1, MAXT), jnp.int32),
            pltpu.VMEM((1, MAXT), jnp.int32),
            pltpu.VMEM((FEAT, 2048), jnp.bfloat16),
            pltpu.VMEM((NV, 2048), jnp.float32),
        ] + [pltpu.VMEM((n, ROWS, 16, 128), jnp.bfloat16) for n in sizes] + [
            pltpu.VMEM((5, HALF, 5, 16, 128), jnp.bfloat16),
            pltpu.VMEM((5 * HALF, 256, 256), jnp.bfloat16),
            pltpu.VMEM((HALF + 1, 16, 128), jnp.bfloat16),
            pltpu.VMEM((HALF + 1, 32, 128), jnp.bfloat16),
            pltpu.VMEM((5 * HALF, 24, 128), jnp.float32),
            pltpu.VMEM((3, HALF, 24, 128), jnp.float32),
            pltpu.VMEM((40, 128), jnp.int32),
            table,
            table,
            pltpu.VMEM((4, 8, 128), jnp.int32),
            pltpu.VMEM((8, 8, 128), jnp.int32),
            pltpu.VMEM((8, 8, 128), jnp.int32),
            table,
            pltpu.VMEM((N_COL, 128), jnp.int32),
            pltpu.SMEM((N_COL, 128), jnp.int32),
            table,
            pltpu.SMEM((8, 128), jnp.int32),
            table,
            pltpu.SMEM((8, 128), jnp.int32),
            pltpu.VMEM((8, 128), jnp.float32),
            pltpu.VMEM((N_COL, 8, 128), jnp.float32),
            pltpu.VMEM((N_ROW, 8, 128), jnp.float32),
            pltpu.VMEM((8, 128), jnp.float32),
            pltpu.SemaphoreType.DMA((N_EVENT,)),
            pltpu.SemaphoreType.DMA((N_EVENT,)),
            pltpu.SemaphoreType.DMA((N_COL + N_ROW,)),
            pltpu.SemaphoreType.DMA((N_COL + N_ROW,)),
            pltpu.SemaphoreType.DMA((N_COL + N_ROW,)),
            pltpu.SemaphoreType.DMA((N_COL + N_ROW,)),
            pltpu.SemaphoreType.DMA((4,)),
        ],
        compiler_params=pltpu.CompilerParams(
            collective_id=0, has_side_effects=True, vmem_limit_bytes=60 * 1024 * 1024
        ),
        name="gather_apply_reduce",
    )(tile_counts, row_blocks, col_blocks, states.T, right_sides)


def shards(states, right_sides, row_blocks, col_blocks, tile_counts):
    applied, coef = iterate(states, right_sides, row_blocks, col_blocks, tile_counts)
    step_size, ratio = coef[:NV, 0:1], coef[:NV, 1:2]
    residual = right_sides - step_size * applied
    return (step_size * right_sides, residual, residual + ratio * right_sides)


def solution(mesh):
    placed = (
        P(("row", "col"), None),
        P(None, ("row", "col")),
        P(("row", "col"), None),
        P(("row", "col"), None),
        P(("row", "col")),
    )
    return jax.shard_map(
        shards,
        mesh=mesh,
        in_specs=placed,
        out_specs=(P(None, ("row", "col")), P(None, ("row", "col")), P(None, ("row", "col"))),
        check_vma=False,
    )
```

```python
import math

import jax
import jax.numpy as jnp
from jax import lax
from jax.experimental import pallas as pl
from jax.experimental.pallas import tpu as pltpu
from jax.sharding import PartitionSpec as P

FEAT = 64
NV = 17
BLK = 128
HALF = 8
N_ROW = 8
N_COL = 32
MAXT = 320

V_AT, W_AT, E_AT, ROWS = 32, 40, 41, 45
PART_A, PART_B = (0, 22), (22, 45)
MESH = pl.DeviceIdType.MESH
COL_ORDER = [*range(16, 24), *range(8, 16), *range(1, 8), *range(24, 32)]
ROW_ORDER = [4, 3, 5, 2, 6, 1, 7]
NN = (((1,), (0,)), ((), ()))
NT = (((1,), (1,)), ((), ()))
rate = math.sqrt(5.0) * math.log2(math.e)
quad = math.log(2.0) ** 2 / 3.0
lin = math.log(2.0)


def dot(a, b, dims):
    return lax.dot_general(a, b, dims, preferred_element_type=jnp.float32)


def matern(squared):
    kept = jnp.maximum(squared, 1e-30)
    z = (kept * lax.rsqrt(kept)) * (-rate)
    return (((z * quad - lin) * z + 1.0) * jnp.exp2(z)).astype(jnp.bfloat16)


def split3(value):
    high = value.astype(jnp.bfloat16).astype(jnp.float32)
    rest = value - high
    middle = rest.astype(jnp.bfloat16).astype(jnp.float32)
    return high, middle, rest - middle


SOURCE_GROUPS = (((0, 0), (0, 1)), ((1, 0), (3, 0)), ((1, 1), (3, 1)), ((2, 0), (2, 1)))
PLACE = {slot: (g, at) for g, group in enumerate(SOURCE_GROUPS) for at, slot in enumerate(group)}
OUTPUTS = (0, 1, 3, 2)
STACK = 4


class Plan:
    def __init__(self):
        self.events = {}
        for m in (1, 3, 2):
            self.add("x%d" % m, "source", 0, (0, ROWS), m)
            self.add("y%d" % m, "output", 0, None, m)
            self.add("r%d" % m, "return", m, None, m)
        for dx in range(4):
            self.add("s%d" % dx, "sibling", dx, (0, ROWS), 0)
        for part, rows in (("a", PART_A), ("b", PART_B)):
            for step in range(3):
                self.add("u%d%s" % (step + 1, part), "stack", step, rows, 1)
                self.add("d%d%s" % (step + 1, part), "stack", (8 - step) % 8, rows, 7)
        self.add("u4a", "stack", 2, PART_A, 2)
        self.add("d4b", "stack", 6, PART_B, 6)

    def add(self, name, *what):
        self.events[name] = (len(self.events),) + what


PLAN = Plan()
N_EVENT = len(PLAN.events)


def names(text):
    return text.split()


ROUND0 = names("s0 x1 x3 y1") + names("y3 u1a d1a") + names("u1b d1b")
Z1 = [("u1a", "u2a"), ("d1a", "d2a"), ("u1b", "u2b"), ("d1b", "d2b")]
Z2A = [("u2a", "u3a u4a"), ("d2a", "d3a")]
Z2B = [("d2b", "d4b d3b"), ("u2b", "u3b")]


def kernel(
    count_ref, u_hbm, v_hbm, states_hbm, sides_hbm,
    applied_hbm, coef_ref,
    applied_ref, u_ref, v_ref, states_ref, sides_ref, buf0, buf1, buf2, buf3, bufz, turned_ref, weights, mask_e, mask_v, acc, part_in,
    mine_ref, theirs_ref, wide_ref, prow, qrow, zrow, qall, ptab, ptab_smem, first_tab, first_smem, last_tab, last_smem,
    stat_out, stat1, stat2, stat2_out,
    ssem, rsem, tab_ssem, tab_rsem, st_ssem, st_rsem, local_sem,
):
    z = lax.axis_index("row")
    c = lax.axis_index("col")
    cy, cx, ck = c // 8, (c // 2) % 4, c % 2
    bufs = (buf0, buf1, buf2, buf3)
    spot = 2 * cx + ck
    load_states = pltpu.make_async_copy(states_hbm, states_ref, local_sem.at[0])
    load_sides = pltpu.make_async_copy(sides_hbm, sides_ref, local_sem.at[1])
    load_u = pltpu.make_async_copy(u_hbm, u_ref, local_sem.at[2])
    load_v = pltpu.make_async_copy(v_hbm, v_ref, local_sem.at[3])
    load_states.start()
    load_sides.start()
    load_u.start()
    load_v.start()

    def col_of(dx, dy, dk):
        other = (ck + 1) % 2 if dk else ck
        return (((cy + dy) % 4) * 4 + (cx + dx) % 4) * 2 + other

    barrier = pltpu.get_barrier_semaphore()

    def greet_col(o, carry):
        pl.semaphore_signal(barrier, inc=1, device_id=(z, (c + o) % N_COL), device_id_type=MESH)
        return carry

    def greet_row(o, carry):
        pl.semaphore_signal(barrier, inc=1, device_id=((z + o) % N_ROW, c), device_id_type=MESH)
        return carry

    lax.fori_loop(1, N_COL, greet_col, 0)
    lax.fori_loop(1, N_ROW, greet_row, 0)

    def copy(name):
        index, kind, slot, rows, move = PLAN.events[name]
        span = None if rows is None else pl.ds(rows[0], rows[1] - rows[0])
        if kind == "stack":
            src = bufz.at[slot, span]
            dst = bufz.at[(slot + move) % 8, span]
            target = ((z + move) % N_ROW, c)
        elif kind == "source":
            src = buf0.at[0, span]
            to_g, to_at = PLACE[move, 0]
            dst = bufs[to_g].at[to_at, span]
            target = (z, col_of(move, 0, 0))
        elif kind == "sibling":
            g, at = PLACE[slot, 0]
            to_g, to_at = PLACE[slot, 1]
            src = bufs[g].at[at, span]
            dst = bufs[to_g].at[to_at, span]
            target = (z, col_of(0, 0, 1))
        elif kind == "output":
            src = turned_ref.at[0]
            dst = turned_ref.at[OUTPUTS.index(move)]
            target = (z, col_of(0, move, 0))
        else:
            src = acc.at[pl.ds(8 * OUTPUTS.index(slot), 8)]
            dst = part_in.at[OUTPUTS.index(slot) - 1]
            target = (z, col_of(0, -move, 0))
        return pltpu.make_async_remote_copy(
            src_ref=src, dst_ref=dst, send_sem=ssem.at[index], recv_sem=rsem.at[index],
            device_id=target, device_id_type=MESH,
        )

    def run(entries):
        for waits, starts in entries:
            for name in names(waits):
                copy(name).wait_recv()
            for name in names(starts):
                copy(name).start()

    t16 = lax.broadcasted_iota(jnp.int32, (16, 256), 0)
    n16 = lax.broadcasted_iota(jnp.int32, (16, 256), 1)
    ones16 = ((t16 < 3) & (n16 < 128)) | ((t16 >= 3) & (t16 < 6) & (n16 >= 128))
    ones16 = jnp.where(ones16, 1.0, 0.0).astype(jnp.bfloat16)
    row16 = lax.broadcasted_iota(jnp.int32, (16, 128), 0)
    load_states.wait()
    load_sides.wait()
    lane64 = lax.broadcasted_iota(jnp.int32, (64, 128), 1)
    for base, chunk in ((0, buf0), (HALF, bufz)):
        tail = jnp.where(lane64 % 16 // 3 == 2, 1.0, 0.0)
        for j in range(HALF):
            b = base + j
            turned = states_ref[:, b * BLK:(b + 1) * BLK].astype(jnp.float32)
            own_turned = turned_ref.at[0 if base == 0 else STACK, j]
            own_turned[0:4] = (turned * -2.0).astype(jnp.bfloat16).reshape(4, 16, 128)
            small = jnp.zeros((16, 128), jnp.float32)
            for k, piece in enumerate(split3(jnp.sum(turned * turned, axis=0, keepdims=True))):
                small = jnp.where(row16 == 6 + k, piece, small)
            own_turned[4] = small.astype(jnp.bfloat16)
            block = turned.T
            feats = jnp.concatenate([block[:64], block[64:]], axis=1).astype(jnp.bfloat16)
            chunk[0, 4 * j:4 * j + 4] = feats.reshape(4, 16, 128)
            total = jnp.sum(block * block, axis=1, keepdims=True)
            for k, piece in enumerate(split3(total)):
                tail = jnp.where(lane64 == 16 * j + k, piece[:64], tail)
                tail = jnp.where(lane64 == 16 * j + 3 + k, piece[64:], tail)
            sides = sides_ref[:, b * BLK:(b + 1) * BLK]
            chunk[0, V_AT + j] = sides[:16].astype(jnp.bfloat16)
        last = [sides_ref[16:17, (base + j) * BLK:(base + j + 1) * BLK] for j in range(HALF)]
        last = jnp.concatenate(last + [jnp.zeros((8, 128), jnp.float32)], axis=0)
        chunk[0, W_AT] = last.astype(jnp.bfloat16)
        chunk[0, E_AT:E_AT + 4] = tail.astype(jnp.bfloat16).reshape(4, 16, 128)

    load_u.wait()
    load_v.wait()
    u, v = u_ref[...], v_ref[...]
    live = lax.broadcasted_iota(jnp.int32, (1, MAXT), 1) < count_ref[0]
    line = (u & 15) < HALF
    own = jnp.where(line, v & 15, (u & 15) - HALF)
    other = jnp.where(line, u & 15, (v & 15) - HALF)
    partner = jnp.where(live, jnp.where(line, u >> 4, N_COL + (v >> 4)), -1)
    hit = lax.broadcasted_iota(jnp.int32, (40, MAXT), 0) == partner
    lane40 = lax.broadcasted_iota(jnp.int32, (40, 128), 1)
    mine = jnp.zeros((40, 128), jnp.int32)
    theirs = jnp.zeros((40, 128), jnp.int32)
    for i in range(HALF):
        here = jnp.sum(jnp.where(hit & (own == i), other + 1, 0), axis=1, keepdims=True)
        there = jnp.sum(jnp.where(hit & (other == i), own + 1, 0), axis=1, keepdims=True)
        mine = jnp.where(lane40 == i, here, mine)
        theirs = jnp.where(lane40 == i, there, theirs)
    mine_ref[...] = mine
    theirs_ref[...] = theirs[N_COL:]
    wide = theirs[0:8]
    for y in range(1, 4):
        wide = wide + pltpu.roll(theirs[8 * y:8 * y + 8], 8 * y, 1)
    wide_ref[...] = wide
    qrow[spot] = wide
    zrow[z] = theirs[N_COL:]
    prow[0] = mine_ref[pl.ds(pl.multiple_of(8 * cy, 8), 8), :]

    zero64 = jnp.zeros((64, 128), jnp.bfloat16)

    def weigh(slot):
        for j in range(HALF):
            at = 8 * slot + j
            scaled = turned_ref[slot, j, 0:4].reshape(64, 128)
            weights[at, 0:64, :] = jnp.concatenate([scaled, zero64], axis=1)
            weights[at, 64:128, :] = jnp.concatenate([zero64, scaled], axis=1)
            strip = turned_ref[slot, j, 4]
            small = jnp.concatenate([strip, strip], axis=1) + ones16
            for k in range(HALF):
                weights[at, 128 + 16 * k:144 + 16 * k, :] = small

    weigh(0)
    lane16 = lax.broadcasted_iota(jnp.int32, (16, 128), 1)
    row32 = lax.broadcasted_iota(jnp.int32, (32, 128), 0)
    for p in range(HALF + 1):
        mask_e[p] = jnp.where(lane16 // 16 == p - 1, 1.0, 0.0).astype(jnp.bfloat16)
        keep = (row32 < 16) | (row32 == 16 + p - 1) if p else row32 < 0
        mask_v[p] = jnp.where(keep, 1.0, 0.0).astype(jnp.bfloat16)

    pl.semaphore_wait(barrier, N_COL + N_ROW - 2)

    def share(src, dst, along_col, method):
        offsets = COL_ORDER if along_col else ROW_ORDER
        for o in offsets:
            if along_col:
                to, slot, sem = (z, (c + o) % N_COL), c, o
            else:
                to, slot, sem = ((z + o) % N_ROW, c), z, N_COL + o
            d = pltpu.make_async_remote_copy(
                src_ref=src, dst_ref=dst.at[slot], send_sem=st_ssem.at[sem], recv_sem=st_rsem.at[sem],
                device_id=to, device_id_type=MESH)
            getattr(d, method)()

    def table(kind, method):
        if kind == "y":
            moves = [(20 + m, m, 0, 0) for m in (1, 3, 2)]
        elif kind == "x":
            moves = [(2 * m + k, 0, m, k) for m in (1, 3, 2) for k in range(2)]
        elif kind == "sibling":
            moves = [(1, 0, 0, 1)]
        else:
            moves = []
            for o in (4, 3, 5, 2, 6, 1, 7):
                getattr(pltpu.make_async_remote_copy(
                    src_ref=theirs_ref, dst_ref=zrow.at[z], send_sem=tab_ssem.at[8 + o],
                    recv_sem=tab_rsem.at[8 + o], device_id=((z + o) % N_ROW, c),
                    device_id_type=MESH), method)()
        for index, my, mx, mk in moves:
            if kind == "y":
                src = mine_ref.at[pl.ds(pl.multiple_of(8 * ((cy + my) % 4), 8), 8)]
                dst = prow.at[my]
            else:
                src, dst = wide_ref, qrow.at[spot]
            getattr(pltpu.make_async_remote_copy(
                src_ref=src, dst_ref=dst, send_sem=tab_ssem.at[index], recv_sem=tab_rsem.at[index],
                device_id=(z, col_of(mx, my, mk)), device_id_type=MESH), method)()

    KINDS = ("sibling", "x", "y", "z")
    for kind in KINDS:
        table(kind, "start")
    for name in ROUND0:
        copy(name).start()

    def pairs(dy):
        shift = (128 - 8 * ((cy + 4 - dy) % 4)) % 128
        return jnp.maximum(prow[dy], pltpu.roll(qall[...], shift, 1))

    def source_row(dx, dk):
        return 2 * ((cx + 4 - dx) % 4) + ((ck + 1) % 2 if dk else ck)

    def group(sources, tab, rows, base, outputs, add, unroll, inside):
        def one(i):
            right = weights[base + i]
            first_row = 0 if base == STACK * HALF else base + i - i % HALF
            parts, sides = [], []
            for (buf, slot), row in zip(sources, rows):
                p = tab[row + first_row, i % HALF]
                at = jnp.maximum(p - 1, 0)
                chosen = mask_e[p]
                for k in range(4):
                    parts.append(jnp.concatenate([buf[slot, at * 4 + k], buf[slot, E_AT + k] * chosen], axis=1))
                sides.append(jnp.concatenate([buf[slot, V_AT + at], buf[slot, W_AT]], axis=0) * mask_v[p])
            tiles = matern(dot(jnp.concatenate(parts, axis=0), right, NN))
            stacked = [
                tiles[64 * s:64 * s + 64, 128 * h:128 * h + 128] for s in range(len(sources)) for h in range(2)
            ]
            out = dot(jnp.concatenate(sides, axis=1), jnp.concatenate(stacked, axis=0), NN)
            last = jnp.sum(out[16:24], axis=0, keepdims=True)
            out = jnp.concatenate([out[:16], jnp.broadcast_to(last, (8, 128))], axis=0)
            if add:
                acc[base + i] += out
            else:
                acc[base + i] = out

        def body(turn, carry):
            for at, entries in inside.items():
                @pl.when(turn == at)
                def _():
                    run(entries)
            for step in range(unroll):
                one(unroll * turn + step)
            return carry

        lax.fori_loop(0, outputs * HALF // unroll, body, 0)

    def of_groups(*which):
        sources = [(bufs[g], at) for g in which for at in range(2)]
        rows = [source_row(dx, dk) for g in which for dx, dk in SOURCE_GROUPS[g]]
        return sources, rows

    for row in range(8):
        qall[row:row + 1, :] = jnp.zeros((1, 128), jnp.int32)
    sibling_row = source_row(0, 1)
    table("sibling", "wait_recv")
    qall[pl.ds(spot, 1), :] = qrow[spot, pl.ds(spot, 1), :]
    qall[pl.ds(sibling_row, 1), :] = qrow[sibling_row, pl.ds(spot, 1), :]
    first_tab[...] = pairs(0)
    to_smem = pltpu.make_async_copy(first_tab, first_smem, local_sem.at[0])
    to_smem.start()
    to_smem.wait()
    run([("s0", "")])
    sources, rows = of_groups(0)
    group(sources, first_smem, rows, 0, 1, False, 8, {})
    run([("", "x2 y2")])

    for kind in ("x", "y"):
        table(kind, "wait_recv")
    for row in range(8):
        qall[row:row + 1, :] = qrow[row, pl.ds(spot, 1), :]
    for k, dy in enumerate(OUTPUTS):
        ptab[8 * k:8 * k + 8, :] = pairs(dy)
    to_smem = pltpu.make_async_copy(ptab, ptab_smem, local_sem.at[0])
    to_smem.start()
    to_smem.wait()
    weigh(STACK)

    run(Z1)
    run([("x1", "s1"), ("x3", "s3")])
    sources, rows = of_groups(1)
    group(sources, ptab_smem, rows, 0, 1, True, 8, {})

    table("z", "wait_recv")
    for row in range(8):
        qall[row:row + 1, :] = zrow[row, pl.ds(z, 1), :]
    last_tab[...] = jnp.maximum(mine_ref[N_COL:, :], qall[...])
    to_smem = pltpu.make_async_copy(last_tab, last_smem, local_sem.at[1])
    to_smem.start()

    run([("y1", "")])
    weigh(1)
    run([("s1 s3", "")])
    sources, rows = of_groups(0, 1, 2)
    group(sources, ptab_smem, rows, HALF, 1, False, 4, {1: Z2A + [("x2", "s2")]})
    run(Z2B)
    sources, rows = of_groups(2)
    group(sources, ptab_smem, rows, 0, 1, True, 8, {})
    run([("s2 y2", "")])
    weigh(3)
    sources, rows = of_groups(0, 1, 2, 3)
    group(sources, ptab_smem, rows, 3 * HALF, 1, False, 4, {})
    last_sources, last_rows = of_groups(3)
    run([("y3", "r2")])
    group(last_sources, ptab_smem, last_rows, HALF, 1, True, 8, {})
    run([("", "r1")])
    weigh(2)
    group(sources, ptab_smem, rows, 2 * HALF, 1, False, 4, {})
    run([("", "r3")])
    group(last_sources, ptab_smem, last_rows, 0, 1, True, 8, {})
    run([("u3a u3b u4a", ""), ("d3a d3b d4b", "")])
    to_smem.wait()
    stack_rows = [(z + N_ROW - d) % N_ROW for d in range(N_ROW)]
    group([(bufz, d) for d in range(N_ROW)], last_smem, stack_rows, STACK * HALF, 1, False, 4, {})
    run([("r1 r3 r2", "")])

    old = jnp.zeros((NV, 128), jnp.float32)
    curve = jnp.zeros((NV, 128), jnp.float32)
    for b in range(2 * HALF):
        product = acc[b if b < HALF else STACK * HALF + b - HALF]
        if b < HALF:
            product = product + part_in[0, b] + part_in[1, b] + part_in[2, b]
        sides = sides_ref[:, b * BLK:(b + 1) * BLK]
        applied = sides + product[:NV]
        applied_ref[:, b * BLK:(b + 1) * BLK] = applied
        old += sides * sides
        curve += sides * applied
    save = pltpu.make_async_copy(applied_ref, applied_hbm, local_sem.at[0])
    save.start()
    old = jnp.sum(old, axis=1, keepdims=True)
    curve = jnp.sum(curve, axis=1, keepdims=True)
    centre = jnp.where(curve > 0.0, jnp.minimum(old / curve, 1.0), 1.0)
    n_sum = jnp.zeros((NV, 128), jnp.float32)
    d_sum = jnp.zeros((NV, 128), jnp.float32)
    q_sum = jnp.zeros((NV, 128), jnp.float32)
    for b in range(2 * HALF):
        applied = applied_ref[:, b * BLK:(b + 1) * BLK]
        left = sides_ref[:, b * BLK:(b + 1) * BLK] - centre * applied
        n_sum += left * left
        d_sum += left * applied
        q_sum += applied * applied
    columns = [old, curve] + [jnp.sum(s, axis=1, keepdims=True) for s in (n_sum, d_sum, q_sum)] + [centre]
    lane17 = lax.broadcasted_iota(jnp.int32, (NV, 128), 1)
    packed = jnp.zeros((NV, 128), jnp.float32)
    for k, column in enumerate(columns):
        packed = jnp.where(lane17 == k, column, packed)
    packed = jnp.concatenate([packed, jnp.zeros((128 - NV, 128), jnp.float32)], axis=0)
    mine_stats = packed.T[0:8]

    def merge(stats):
        total = jnp.sum(stats, axis=0)
        old, curve, q = total[0:1], total[1:2], total[4:5]
        ratio = old / curve
        centre = jnp.where(curve > 0.0, jnp.minimum(ratio, 1.0), 1.0)

        def moved(to):
            eps = to - stats[:, 5:6, :]
            n = stats[:, 2:3, :] - 2.0 * eps * stats[:, 3:4, :] + eps * eps * stats[:, 4:5, :]
            return jnp.sum(n, axis=0), jnp.sum(stats[:, 3:4, :] - eps * stats[:, 4:5, :], axis=0)

        return old, curve, q, ratio, centre, moved

    stat_out[...] = mine_stats
    stat1[c] = mine_stats
    share(stat_out, stat1, True, "start")
    for name in PLAN.events:
        copy(name).wait_send()
    for kind in KINDS:
        table(kind, "wait_send")
    share(stat_out, stat1, True, "wait_recv")
    old, curve, q, ratio, centre, moved = merge(stat1[...])
    n, d = moved(centre)
    row_stats = jnp.concatenate([old, curve, n, d, q, centre, old, old], axis=0)
    stat2_out[...] = row_stats
    stat2[z] = row_stats
    share(stat2_out, stat2, False, "start")
    share(stat_out, stat1, True, "wait_send")
    share(stat2_out, stat2, False, "wait_recv")
    old, curve, q, ratio, centre, moved = merge(stat2[...])
    n, d = moved(ratio)
    pair = jnp.concatenate([ratio, n / old, jnp.zeros((126, 128), jnp.float32)], axis=0)
    coef_ref[...] = pair.T[0:24]
    save.wait()

    share(stat2_out, stat2, False, "wait_send")


def iterate(states, right_sides, row_blocks, col_blocks, tile_counts):
    vmem = pl.BlockSpec(memory_space=pltpu.VMEM)
    hbm = pl.BlockSpec(memory_space=pltpu.HBM)
    sizes = [len(group) for group in SOURCE_GROUPS] + [N_ROW]
    table = pltpu.VMEM((8, 128), jnp.int32)
    return pl.pallas_call(
        kernel,
        out_shape=(
            jax.ShapeDtypeStruct((NV, 2048), jnp.float32),
            jax.ShapeDtypeStruct((24, 128), jnp.float32),
        ),
        in_specs=[pl.BlockSpec(memory_space=pltpu.SMEM), hbm, hbm, hbm, hbm],
        out_specs=(hbm, vmem),
        scratch_shapes=[
            pltpu.VMEM((NV, 2048), jnp.float32),
            pltpu.VMEM((1, MAXT), jnp.int32),
            pltpu.VMEM((1, MAXT), jnp.int32),
            pltpu.VMEM((FEAT, 2048), jnp.bfloat16),
            pltpu.VMEM((NV, 2048), jnp.float32),
        ] + [pltpu.VMEM((n, ROWS, 16, 128), jnp.bfloat16) for n in sizes] + [
            pltpu.VMEM((5, HALF, 5, 16, 128), jnp.bfloat16),
            pltpu.VMEM((5 * HALF, 256, 256), jnp.bfloat16),
            pltpu.VMEM((HALF + 1, 16, 128), jnp.bfloat16),
            pltpu.VMEM((HALF + 1, 32, 128), jnp.bfloat16),
            pltpu.VMEM((5 * HALF, 24, 128), jnp.float32),
            pltpu.VMEM((3, HALF, 24, 128), jnp.float32),
            pltpu.VMEM((40, 128), jnp.int32),
            table,
            table,
            pltpu.VMEM((4, 8, 128), jnp.int32),
            pltpu.VMEM((8, 8, 128), jnp.int32),
            pltpu.VMEM((8, 8, 128), jnp.int32),
            table,
            pltpu.VMEM((N_COL, 128), jnp.int32),
            pltpu.SMEM((N_COL, 128), jnp.int32),
            table,
            pltpu.SMEM((8, 128), jnp.int32),
            table,
            pltpu.SMEM((8, 128), jnp.int32),
            pltpu.VMEM((8, 128), jnp.float32),
            pltpu.VMEM((N_COL, 8, 128), jnp.float32),
            pltpu.VMEM((N_ROW, 8, 128), jnp.float32),
            pltpu.VMEM((8, 128), jnp.float32),
            pltpu.SemaphoreType.DMA((N_EVENT,)),
            pltpu.SemaphoreType.DMA((N_EVENT,)),
            pltpu.SemaphoreType.DMA((N_COL + N_ROW,)),
            pltpu.SemaphoreType.DMA((N_COL + N_ROW,)),
            pltpu.SemaphoreType.DMA((N_COL + N_ROW,)),
            pltpu.SemaphoreType.DMA((N_COL + N_ROW,)),
            pltpu.SemaphoreType.DMA((4,)),
        ],
        compiler_params=pltpu.CompilerParams(
            collective_id=0, has_side_effects=True, vmem_limit_bytes=60 * 1024 * 1024
        ),
        name="gather_apply_reduce",
    )(tile_counts, row_blocks, col_blocks, states.T, right_sides)


def shards(states, right_sides, row_blocks, col_blocks, tile_counts):
    applied, coef = iterate(states, right_sides, row_blocks, col_blocks, tile_counts)
    step_size, ratio = coef[:NV, 0:1], coef[:NV, 1:2]
    residual = right_sides - step_size * applied
    return (step_size * right_sides, residual, residual + ratio * right_sides)


def solution(mesh):
    placed = (
        P(("row", "col"), None),
        P(None, ("row", "col")),
        P(("row", "col"), None),
        P(("row", "col"), None),
        P(("row", "col")),
    )
    return jax.shard_map(
        shards,
        mesh=mesh,
        in_specs=placed,
        out_specs=(P(None, ("row", "col")), P(None, ("row", "col")), P(None, ("row", "col"))),
        check_vma=False,
    )
```

```python
import math

import jax
import jax.numpy as jnp
from jax import lax
from jax.experimental import pallas as pl
from jax.experimental.pallas import tpu as pltpu
from jax.sharding import PartitionSpec as P

FEAT = 64
NV = 17
BLK = 128
HALF = 8
N_ROW = 8
N_COL = 32
MAXT = 320

V_AT, W_AT, E_AT, ROWS = 32, 40, 41, 45
PART_A, PART_B = (0, 22), (22, 45)
MESH = pl.DeviceIdType.MESH
COL_ORDER = [*range(16, 24), *range(8, 16), *range(1, 8), *range(24, 32)]
ROW_ORDER = [4, 3, 5, 2, 6, 1, 7]
NN = (((1,), (0,)), ((), ()))
NT = (((1,), (1,)), ((), ()))
rate = math.sqrt(5.0) * math.log2(math.e)
quad = math.log(2.0) ** 2 / 3.0
lin = math.log(2.0)


def dot(a, b, dims):
    return lax.dot_general(a, b, dims, preferred_element_type=jnp.float32)


def matern(squared):
    kept = jnp.maximum(squared, 1e-30)
    z = (kept * lax.rsqrt(kept)) * (-rate)
    return (((z * quad - lin) * z + 1.0) * jnp.exp2(z)).astype(jnp.bfloat16)


def split3(value):
    high = value.astype(jnp.bfloat16).astype(jnp.float32)
    rest = value - high
    middle = rest.astype(jnp.bfloat16).astype(jnp.float32)
    return high, middle, rest - middle


SOURCE_GROUPS = (((0, 0), (0, 1)), ((1, 0), (3, 0)), ((1, 1), (3, 1)), ((2, 0), (2, 1)))
PLACE = {slot: (g, at) for g, group in enumerate(SOURCE_GROUPS) for at, slot in enumerate(group)}
OUTPUTS = (0, 1, 3, 2)
STACK = 4


class Plan:
    def __init__(self):
        self.events = {}
        for m in (1, 3, 2):
            self.add("x%d" % m, "source", 0, (0, ROWS), m)
            self.add("y%d" % m, "output", 0, None, m)
            self.add("r%d" % m, "return", m, None, m)
        for dx in range(4):
            self.add("s%d" % dx, "sibling", dx, (0, ROWS), 0)
        for part, rows in (("a", PART_A), ("b", PART_B)):
            for step in range(3):
                self.add("u%d%s" % (step + 1, part), "stack", step, rows, 1)
                self.add("d%d%s" % (step + 1, part), "stack", (8 - step) % 8, rows, 7)
        self.add("u4a", "stack", 2, PART_A, 2)
        self.add("d4b", "stack", 6, PART_B, 6)

    def add(self, name, *what):
        self.events[name] = (len(self.events),) + what


PLAN = Plan()
N_EVENT = len(PLAN.events)


def names(text):
    return text.split()


ROUND0 = names("s0 x1 x3 y1") + names("y3 u1a d1a") + names("u1b d1b")
Z1 = [("u1a", "u2a"), ("d1a", "d2a"), ("u1b", "u2b"), ("d1b", "d2b")]
Z2A = [("u2a", "u3a u4a"), ("d2a", "d3a")]
Z2B = [("d2b", "d4b d3b"), ("u2b", "u3b")]


def kernel(
    count_ref, u_hbm, v_hbm, states_hbm, sides_hbm,
    applied_hbm, coef_ref,
    applied_ref, u_ref, v_ref, states_ref, sides_ref, buf0, buf1, buf2, buf3, bufz, turned_ref, weights, mask_e, mask_v, acc, part_in,
    mine_ref, theirs_ref, wide_ref, prow, qrow, zrow, qall, ptab, ptab_smem, first_tab, first_smem, last_tab, last_smem,
    stat_out, stat1, stat2, stat2_out,
    ssem, rsem, tab_ssem, tab_rsem, st_ssem, st_rsem, local_sem,
):
    z = lax.axis_index("row")
    c = lax.axis_index("col")
    cy, cx, ck = c // 8, (c // 2) % 4, c % 2
    bufs = (buf0, buf1, buf2, buf3)
    spot = 2 * cx + ck
    load_states = pltpu.make_async_copy(states_hbm, states_ref, local_sem.at[0])
    load_sides = pltpu.make_async_copy(sides_hbm, sides_ref, local_sem.at[1])
    load_u = pltpu.make_async_copy(u_hbm, u_ref, local_sem.at[2])
    load_v = pltpu.make_async_copy(v_hbm, v_ref, local_sem.at[3])
    load_states.start()
    load_sides.start()
    load_u.start()
    load_v.start()

    def col_of(dx, dy, dk):
        other = (ck + 1) % 2 if dk else ck
        return (((cy + dy) % 4) * 4 + (cx + dx) % 4) * 2 + other

    barrier = pltpu.get_barrier_semaphore()

    def greet_col(o, carry):
        pl.semaphore_signal(barrier, inc=1, device_id=(z, (c + o) % N_COL), device_id_type=MESH)
        return carry

    def greet_row(o, carry):
        pl.semaphore_signal(barrier, inc=1, device_id=((z + o) % N_ROW, c), device_id_type=MESH)
        return carry

    lax.fori_loop(1, N_COL, greet_col, 0)
    lax.fori_loop(1, N_ROW, greet_row, 0)

    def copy(name):
        index, kind, slot, rows, move = PLAN.events[name]
        span = None if rows is None else pl.ds(rows[0], rows[1] - rows[0])
        if kind == "stack":
            src = bufz.at[slot, span]
            dst = bufz.at[(slot + move) % 8, span]
            target = ((z + move) % N_ROW, c)
        elif kind == "source":
            src = buf0.at[0, span]
            to_g, to_at = PLACE[move, 0]
            dst = bufs[to_g].at[to_at, span]
            target = (z, col_of(move, 0, 0))
        elif kind == "sibling":
            g, at = PLACE[slot, 0]
            to_g, to_at = PLACE[slot, 1]
            src = bufs[g].at[at, span]
            dst = bufs[to_g].at[to_at, span]
            target = (z, col_of(0, 0, 1))
        elif kind == "output":
            src = turned_ref.at[0]
            dst = turned_ref.at[OUTPUTS.index(move)]
            target = (z, col_of(0, move, 0))
        else:
            src = acc.at[pl.ds(8 * OUTPUTS.index(slot), 8)]
            dst = part_in.at[OUTPUTS.index(slot) - 1]
            target = (z, col_of(0, -move, 0))
        return pltpu.make_async_remote_copy(
            src_ref=src, dst_ref=dst, send_sem=ssem.at[index], recv_sem=rsem.at[index],
            device_id=target, device_id_type=MESH,
        )

    def run(entries):
        for waits, starts in entries:
            for name in names(waits):
                copy(name).wait_recv()
            for name in names(starts):
                copy(name).start()

    t16 = lax.broadcasted_iota(jnp.int32, (16, 256), 0)
    n16 = lax.broadcasted_iota(jnp.int32, (16, 256), 1)
    ones16 = ((t16 < 3) & (n16 < 128)) | ((t16 >= 3) & (t16 < 6) & (n16 >= 128))
    ones16 = jnp.where(ones16, 1.0, 0.0).astype(jnp.bfloat16)
    row16 = lax.broadcasted_iota(jnp.int32, (16, 128), 0)
    load_states.wait()
    load_sides.wait()
    lane64 = lax.broadcasted_iota(jnp.int32, (64, 128), 1)
    for base, chunk in ((0, buf0), (HALF, bufz)):
        tail = jnp.where(lane64 % 16 // 3 == 2, 1.0, 0.0)
        for j in range(HALF):
            b = base + j
            turned = states_ref[:, b * BLK:(b + 1) * BLK].astype(jnp.float32)
            own_turned = turned_ref.at[0 if base == 0 else STACK, j]
            own_turned[0:4] = (turned * -2.0).astype(jnp.bfloat16).reshape(4, 16, 128)
            small = jnp.zeros((16, 128), jnp.float32)
            for k, piece in enumerate(split3(jnp.sum(turned * turned, axis=0, keepdims=True))):
                small = jnp.where(row16 == 6 + k, piece, small)
            own_turned[4] = small.astype(jnp.bfloat16)
            block = turned.T
            feats = jnp.concatenate([block[:64], block[64:]], axis=1).astype(jnp.bfloat16)
            chunk[0, 4 * j:4 * j + 4] = feats.reshape(4, 16, 128)
            total = jnp.sum(block * block, axis=1, keepdims=True)
            for k, piece in enumerate(split3(total)):
                tail = jnp.where(lane64 == 16 * j + k, piece[:64], tail)
                tail = jnp.where(lane64 == 16 * j + 3 + k, piece[64:], tail)
            sides = sides_ref[:, b * BLK:(b + 1) * BLK]
            chunk[0, V_AT + j] = sides[:16].astype(jnp.bfloat16)
        last = [sides_ref[16:17, (base + j) * BLK:(base + j + 1) * BLK] for j in range(HALF)]
        last = jnp.concatenate(last + [jnp.zeros((8, 128), jnp.float32)], axis=0)
        chunk[0, W_AT] = last.astype(jnp.bfloat16)
        chunk[0, E_AT:E_AT + 4] = tail.astype(jnp.bfloat16).reshape(4, 16, 128)

    load_u.wait()
    load_v.wait()
    u, v = u_ref[...], v_ref[...]
    live = lax.broadcasted_iota(jnp.int32, (1, MAXT), 1) < count_ref[0]
    line = (u & 15) < HALF
    own = jnp.where(line, v & 15, (u & 15) - HALF)
    other = jnp.where(line, u & 15, (v & 15) - HALF)
    partner = jnp.where(live, jnp.where(line, u >> 4, N_COL + (v >> 4)), -1)
    hit = lax.broadcasted_iota(jnp.int32, (40, MAXT), 0) == partner
    lane40 = lax.broadcasted_iota(jnp.int32, (40, 128), 1)
    mine = jnp.zeros((40, 128), jnp.int32)
    theirs = jnp.zeros((40, 128), jnp.int32)
    for i in range(HALF):
        here = jnp.sum(jnp.where(hit & (own == i), other + 1, 0), axis=1, keepdims=True)
        there = jnp.sum(jnp.where(hit & (other == i), own + 1, 0), axis=1, keepdims=True)
        mine = jnp.where(lane40 == i, here, mine)
        theirs = jnp.where(lane40 == i, there, theirs)
    mine_ref[...] = mine
    theirs_ref[...] = theirs[N_COL:]
    wide = theirs[0:8]
    for y in range(1, 4):
        wide = wide + pltpu.roll(theirs[8 * y:8 * y + 8], 8 * y, 1)
    wide_ref[...] = wide
    qrow[spot] = wide
    zrow[z] = theirs[N_COL:]
    prow[0] = mine_ref[pl.ds(pl.multiple_of(8 * cy, 8), 8), :]

    zero64 = jnp.zeros((64, 128), jnp.bfloat16)

    def weigh(slot):
        for j in range(HALF):
            at = 8 * slot + j
            scaled = turned_ref[slot, j, 0:4].reshape(64, 128)
            weights[at, 0:64, :] = jnp.concatenate([scaled, zero64], axis=1)
            weights[at, 64:128, :] = jnp.concatenate([zero64, scaled], axis=1)
            strip = turned_ref[slot, j, 4]
            small = jnp.concatenate([strip, strip], axis=1) + ones16
            for k in range(HALF):
                weights[at, 128 + 16 * k:144 + 16 * k, :] = small

    weigh(0)
    lane16 = lax.broadcasted_iota(jnp.int32, (16, 128), 1)
    row32 = lax.broadcasted_iota(jnp.int32, (32, 128), 0)
    for p in range(HALF + 1):
        mask_e[p] = jnp.where(lane16 // 16 == p - 1, 1.0, 0.0).astype(jnp.bfloat16)
        keep = (row32 < 16) | (row32 == 16 + p - 1) if p else row32 < 0
        mask_v[p] = jnp.where(keep, 1.0, 0.0).astype(jnp.bfloat16)

    pl.semaphore_wait(barrier, N_COL + N_ROW - 2)

    def share(src, dst, along_col, method):
        offsets = COL_ORDER if along_col else ROW_ORDER
        for o in offsets:
            if along_col:
                to, slot, sem = (z, (c + o) % N_COL), c, o
            else:
                to, slot, sem = ((z + o) % N_ROW, c), z, N_COL + o
            d = pltpu.make_async_remote_copy(
                src_ref=src, dst_ref=dst.at[slot], send_sem=st_ssem.at[sem], recv_sem=st_rsem.at[sem],
                device_id=to, device_id_type=MESH)
            getattr(d, method)()

    def table(kind, method):
        if kind == "y":
            moves = [(20 + m, m, 0, 0) for m in (1, 3, 2)]
        elif kind == "x":
            moves = [(2 * m + k, 0, m, k) for m in (1, 3, 2) for k in range(2)]
        elif kind == "sibling":
            moves = [(1, 0, 0, 1)]
        else:
            moves = []
            for o in (4, 3, 5, 2, 6, 1, 7):
                getattr(pltpu.make_async_remote_copy(
                    src_ref=theirs_ref, dst_ref=zrow.at[z], send_sem=tab_ssem.at[8 + o],
                    recv_sem=tab_rsem.at[8 + o], device_id=((z + o) % N_ROW, c),
                    device_id_type=MESH), method)()
        for index, my, mx, mk in moves:
            if kind == "y":
                src = mine_ref.at[pl.ds(pl.multiple_of(8 * ((cy + my) % 4), 8), 8)]
                dst = prow.at[my]
            else:
                src, dst = wide_ref, qrow.at[spot]
            getattr(pltpu.make_async_remote_copy(
                src_ref=src, dst_ref=dst, send_sem=tab_ssem.at[index], recv_sem=tab_rsem.at[index],
                device_id=(z, col_of(mx, my, mk)), device_id_type=MESH), method)()

    KINDS = ("sibling", "x", "y", "z")
    for kind in ("sibling", "x"):
        table(kind, "start")
    for name in ROUND0[:3]:
        copy(name).start()
    table("y", "start")
    for name in ROUND0[3:]:
        copy(name).start()
    table("z", "start")

    def pairs(dy):
        shift = (128 - 8 * ((cy + 4 - dy) % 4)) % 128
        return jnp.maximum(prow[dy], pltpu.roll(qall[...], shift, 1))

    def source_row(dx, dk):
        return 2 * ((cx + 4 - dx) % 4) + ((ck + 1) % 2 if dk else ck)

    def group(sources, tab, rows, base, outputs, add, unroll, inside):
        def one(i):
            right = weights[base + i]
            first_row = 0 if base == STACK * HALF else base + i - i % HALF
            parts, sides = [], []
            for (buf, slot), row in zip(sources, rows):
                p = tab[row + first_row, i % HALF]
                at = jnp.maximum(p - 1, 0)
                chosen = mask_e[p]
                for k in range(4):
                    parts.append(jnp.concatenate([buf[slot, at * 4 + k], buf[slot, E_AT + k] * chosen], axis=1))
                sides.append(jnp.concatenate([buf[slot, V_AT + at], buf[slot, W_AT]], axis=0) * mask_v[p])
            tiles = matern(dot(jnp.concatenate(parts, axis=0), right, NN))
            stacked = [
                tiles[64 * s:64 * s + 64, 128 * h:128 * h + 128] for s in range(len(sources)) for h in range(2)
            ]
            out = dot(jnp.concatenate(sides, axis=1), jnp.concatenate(stacked, axis=0), NN)
            last = jnp.sum(out[16:24], axis=0, keepdims=True)
            out = jnp.concatenate([out[:16], jnp.broadcast_to(last, (8, 128))], axis=0)
            if add:
                acc[base + i] += out
            else:
                acc[base + i] = out

        def body(turn, carry):
            for at, entries in inside.items():
                @pl.when(turn == at)
                def _():
                    run(entries)
            for step in range(unroll):
                one(unroll * turn + step)
            return carry

        lax.fori_loop(0, outputs * HALF // unroll, body, 0)

    def of_groups(*which):
        sources = [(bufs[g], at) for g in which for at in range(2)]
        rows = [source_row(dx, dk) for g in which for dx, dk in SOURCE_GROUPS[g]]
        return sources, rows

    for row in range(8):
        qall[row:row + 1, :] = jnp.zeros((1, 128), jnp.int32)
    sibling_row = source_row(0, 1)
    table("sibling", "wait_recv")
    qall[pl.ds(spot, 1), :] = qrow[spot, pl.ds(spot, 1), :]
    qall[pl.ds(sibling_row, 1), :] = qrow[sibling_row, pl.ds(spot, 1), :]
    first_tab[...] = pairs(0)
    to_smem = pltpu.make_async_copy(first_tab, first_smem, local_sem.at[0])
    to_smem.start()
    to_smem.wait()
    run([("s0", "")])
    sources, rows = of_groups(0)
    group(sources, first_smem, rows, 0, 1, False, 8, {})
    run([("", "x2 y2")])

    for kind in ("x", "y"):
        table(kind, "wait_recv")
    for row in range(8):
        qall[row:row + 1, :] = qrow[row, pl.ds(spot, 1), :]
    for k, dy in enumerate(OUTPUTS):
        ptab[8 * k:8 * k + 8, :] = pairs(dy)
    to_smem = pltpu.make_async_copy(ptab, ptab_smem, local_sem.at[0])
    to_smem.start()
    to_smem.wait()
    weigh(STACK)

    run(Z1)
    run([("x1", "s1"), ("x3", "s3")])
    sources, rows = of_groups(1)
    group(sources, ptab_smem, rows, 0, 1, True, 8, {})

    table("z", "wait_recv")
    for row in range(8):
        qall[row:row + 1, :] = zrow[row, pl.ds(z, 1), :]
    last_tab[...] = jnp.maximum(mine_ref[N_COL:, :], qall[...])
    to_smem = pltpu.make_async_copy(last_tab, last_smem, local_sem.at[1])
    to_smem.start()

    run([("y1", "")])
    weigh(1)
    run([("s1 s3", "")])
    sources, rows = of_groups(0, 1, 2)
    group(sources, ptab_smem, rows, HALF, 1, False, 4, {1: Z2A + [("x2", "s2")]})
    run(Z2B)
    sources, rows = of_groups(2)
    group(sources, ptab_smem, rows, 0, 1, True, 8, {})
    run([("s2 y2", "")])
    weigh(3)
    sources, rows = of_groups(0, 1, 2, 3)
    group(sources, ptab_smem, rows, 3 * HALF, 1, False, 4, {})
    last_sources, last_rows = of_groups(3)
    run([("y3", "r2")])
    group(last_sources, ptab_smem, last_rows, HALF, 1, True, 8, {})
    run([("", "r1")])
    weigh(2)
    group(sources, ptab_smem, rows, 2 * HALF, 1, False, 4, {})
    run([("", "r3")])
    group(last_sources, ptab_smem, last_rows, 0, 1, True, 8, {})
    run([("u3a u3b u4a", ""), ("d3a d3b d4b", "")])
    to_smem.wait()
    stack_rows = [(z + N_ROW - d) % N_ROW for d in range(N_ROW)]
    group([(bufz, d) for d in range(N_ROW)], last_smem, stack_rows, STACK * HALF, 1, False, 4, {})
    run([("r1 r3 r2", "")])

    old = jnp.zeros((NV, 128), jnp.float32)
    curve = jnp.zeros((NV, 128), jnp.float32)
    for b in range(2 * HALF):
        product = acc[b if b < HALF else STACK * HALF + b - HALF]
        if b < HALF:
            product = product + part_in[0, b] + part_in[1, b] + part_in[2, b]
        sides = sides_ref[:, b * BLK:(b + 1) * BLK]
        applied = sides + product[:NV]
        applied_ref[:, b * BLK:(b + 1) * BLK] = applied
        old += sides * sides
        curve += sides * applied
    save = pltpu.make_async_copy(applied_ref, applied_hbm, local_sem.at[0])
    save.start()
    old = jnp.sum(old, axis=1, keepdims=True)
    curve = jnp.sum(curve, axis=1, keepdims=True)
    centre = jnp.where(curve > 0.0, jnp.minimum(old / curve, 1.0), 1.0)
    n_sum = jnp.zeros((NV, 128), jnp.float32)
    d_sum = jnp.zeros((NV, 128), jnp.float32)
    q_sum = jnp.zeros((NV, 128), jnp.float32)
    for b in range(2 * HALF):
        applied = applied_ref[:, b * BLK:(b + 1) * BLK]
        left = sides_ref[:, b * BLK:(b + 1) * BLK] - centre * applied
        n_sum += left * left
        d_sum += left * applied
        q_sum += applied * applied
    columns = [old, curve] + [jnp.sum(s, axis=1, keepdims=True) for s in (n_sum, d_sum, q_sum)] + [centre]
    lane17 = lax.broadcasted_iota(jnp.int32, (NV, 128), 1)
    packed = jnp.zeros((NV, 128), jnp.float32)
    for k, column in enumerate(columns):
        packed = jnp.where(lane17 == k, column, packed)
    packed = jnp.concatenate([packed, jnp.zeros((128 - NV, 128), jnp.float32)], axis=0)
    mine_stats = packed.T[0:8]

    def merge(stats):
        total = jnp.sum(stats, axis=0)
        old, curve, q = total[0:1], total[1:2], total[4:5]
        ratio = old / curve
        centre = jnp.where(curve > 0.0, jnp.minimum(ratio, 1.0), 1.0)

        def moved(to):
            eps = to - stats[:, 5:6, :]
            n = stats[:, 2:3, :] - 2.0 * eps * stats[:, 3:4, :] + eps * eps * stats[:, 4:5, :]
            return jnp.sum(n, axis=0), jnp.sum(stats[:, 3:4, :] - eps * stats[:, 4:5, :], axis=0)

        return old, curve, q, ratio, centre, moved

    stat_out[...] = mine_stats
    stat1[c] = mine_stats
    share(stat_out, stat1, True, "start")
    for name in PLAN.events:
        copy(name).wait_send()
    for kind in KINDS:
        table(kind, "wait_send")
    share(stat_out, stat1, True, "wait_recv")
    old, curve, q, ratio, centre, moved = merge(stat1[...])
    n, d = moved(centre)
    row_stats = jnp.concatenate([old, curve, n, d, q, centre, old, old], axis=0)
    stat2_out[...] = row_stats
    stat2[z] = row_stats
    share(stat2_out, stat2, False, "start")
    share(stat_out, stat1, True, "wait_send")
    share(stat2_out, stat2, False, "wait_recv")
    old, curve, q, ratio, centre, moved = merge(stat2[...])
    n, d = moved(ratio)
    pair = jnp.concatenate([ratio, n / old, jnp.zeros((126, 128), jnp.float32)], axis=0)
    coef_ref[...] = pair.T[0:24]
    save.wait()

    share(stat2_out, stat2, False, "wait_send")


def iterate(states, right_sides, row_blocks, col_blocks, tile_counts):
    vmem = pl.BlockSpec(memory_space=pltpu.VMEM)
    hbm = pl.BlockSpec(memory_space=pltpu.HBM)
    sizes = [len(group) for group in SOURCE_GROUPS] + [N_ROW]
    table = pltpu.VMEM((8, 128), jnp.int32)
    return pl.pallas_call(
        kernel,
        out_shape=(
            jax.ShapeDtypeStruct((NV, 2048), jnp.float32),
            jax.ShapeDtypeStruct((24, 128), jnp.float32),
        ),
        in_specs=[pl.BlockSpec(memory_space=pltpu.SMEM), hbm, hbm, hbm, hbm],
        out_specs=(hbm, vmem),
        scratch_shapes=[
            pltpu.VMEM((NV, 2048), jnp.float32),
            pltpu.VMEM((1, MAXT), jnp.int32),
            pltpu.VMEM((1, MAXT), jnp.int32),
            pltpu.VMEM((FEAT, 2048), jnp.bfloat16),
            pltpu.VMEM((NV, 2048), jnp.float32),
        ] + [pltpu.VMEM((n, ROWS, 16, 128), jnp.bfloat16) for n in sizes] + [
            pltpu.VMEM((5, HALF, 5, 16, 128), jnp.bfloat16),
            pltpu.VMEM((5 * HALF, 256, 256), jnp.bfloat16),
            pltpu.VMEM((HALF + 1, 16, 128), jnp.bfloat16),
            pltpu.VMEM((HALF + 1, 32, 128), jnp.bfloat16),
            pltpu.VMEM((5 * HALF, 24, 128), jnp.float32),
            pltpu.VMEM((3, HALF, 24, 128), jnp.float32),
            pltpu.VMEM((40, 128), jnp.int32),
            table,
            table,
            pltpu.VMEM((4, 8, 128), jnp.int32),
            pltpu.VMEM((8, 8, 128), jnp.int32),
            pltpu.VMEM((8, 8, 128), jnp.int32),
            table,
            pltpu.VMEM((N_COL, 128), jnp.int32),
            pltpu.SMEM((N_COL, 128), jnp.int32),
            table,
            pltpu.SMEM((8, 128), jnp.int32),
            table,
            pltpu.SMEM((8, 128), jnp.int32),
            pltpu.VMEM((8, 128), jnp.float32),
            pltpu.VMEM((N_COL, 8, 128), jnp.float32),
            pltpu.VMEM((N_ROW, 8, 128), jnp.float32),
            pltpu.VMEM((8, 128), jnp.float32),
            pltpu.SemaphoreType.DMA((N_EVENT,)),
            pltpu.SemaphoreType.DMA((N_EVENT,)),
            pltpu.SemaphoreType.DMA((N_COL + N_ROW,)),
            pltpu.SemaphoreType.DMA((N_COL + N_ROW,)),
            pltpu.SemaphoreType.DMA((N_COL + N_ROW,)),
            pltpu.SemaphoreType.DMA((N_COL + N_ROW,)),
            pltpu.SemaphoreType.DMA((4,)),
        ],
        compiler_params=pltpu.CompilerParams(
            collective_id=0, has_side_effects=True, vmem_limit_bytes=60 * 1024 * 1024
        ),
        name="gather_apply_reduce",
    )(tile_counts, row_blocks, col_blocks, states.T, right_sides)


def shards(states, right_sides, row_blocks, col_blocks, tile_counts):
    applied, coef = iterate(states, right_sides, row_blocks, col_blocks, tile_counts)
    step_size, ratio = coef[:NV, 0:1], coef[:NV, 1:2]
    residual = right_sides - step_size * applied
    return (step_size * right_sides, residual, residual + ratio * right_sides)


def solution(mesh):
    placed = (
        P(("row", "col"), None),
        P(None, ("row", "col")),
        P(("row", "col"), None),
        P(("row", "col"), None),
        P(("row", "col")),
    )
    return jax.shard_map(
        shards,
        mesh=mesh,
        in_specs=placed,
        out_specs=(P(None, ("row", "col")), P(None, ("row", "col")), P(None, ("row", "col"))),
        check_vma=False,
    )
```
